32 devices in a mesh: dp: 8 (over z, y), mp: 4 (over x, core).
Axes of the slice: x: 2, y: 2, z: 4, core: 2. Of those that a mesh axis runs over, the one named last changes fastest.
Arguments:
- activations: bfloat16 [32, 256, 1024], P('dp'), may hold values from -6 to 6
- segments: int32 [32, 256], P('dp'), may hold values from 0 to 2, as said below
- first_gain: float32 [2, 1024], replicated, may hold values from 0.5 to 1.5
- first_shift: float32 [2, 1024], replicated, may hold values from -1.5 to 1.5
- query_weight: bfloat16 [2, 1024, 1024], P(None, None, 'mp'), may hold values from -0.1875 to 0.1875
- key_weight: bfloat16 [2, 1024, 1024], P(None, None, 'mp'), may hold values from -0.1875 to 0.1875
- value_weight: bfloat16 [2, 1024, 1024], P(None, None, 'mp'), may hold values from -0.1875 to 0.1875
- query_bias: float32 [2, 1024], P(None, 'mp'), may hold values from -3 to 3
- value_bias: float32 [2, 1024], P(None, 'mp'), may hold values from -3 to 3
- out_weight: bfloat16 [2, 1024, 1024], P(None, None, 'mp'), may hold values from -0.75 to 0.75
- out_bias: float32 [2, 1024], replicated, may hold values from -1.5 to 1.5
- attend_scale: float32 [2, 1024], replicated, may hold values from 0.25 to 1.75
- second_gain: float32 [2, 1024], replicated, may hold values from 0.5 to 1.5
- second_shift: float32 [2, 1024], replicated, may hold values from -1.5 to 1.5
- up_weight: bfloat16 [2, 1024, 4096], P(None, None, 'mp'), may hold values from -0.1875 to 0.1875
- up_bias: float32 [2, 4096], P(None, 'mp'), may hold values from -1.5 to 1.5
- down_weight: bfloat16 [2, 1024, 4096], P(None, None, 'mp'), may hold values from -0.1875 to 0.1875
- down_bias: float32 [2, 1024], replicated, may hold values from -1.5 to 1.5
- feed_scale: float32 [2, 1024], replicated, may hold values from 0.25 to 1.75
- cotangent: bfloat16 [32, 256, 1024], P('dp'), may hold values from -6 to 6
Outputs:
- result: bfloat16 [32, 256, 1024], P('dp')
- input_grad: float32 [32, 256, 1024], P('dp')
- first_gain_grad: float32 [2, 1024], P(None, 'dp')
- first_shift_grad: float32 [2, 1024], P(None, 'dp')
- query_weight_grad: float32 [2, 1024, 1024], P(None, 'dp', 'mp')
- key_weight_grad: float32 [2, 1024, 1024], P(None, 'dp', 'mp')
- value_weight_grad: float32 [2, 1024, 1024], P(None, 'dp', 'mp')
- query_bias_grad: float32 [2, 1024], P(None, ('mp', 'dp'))
- value_bias_grad: float32 [2, 1024], P(None, ('mp', 'dp'))
- out_weight_grad: float32 [2, 1024, 1024], P(None, 'dp', 'mp')
- out_bias_grad: float32 [2, 1024], P(None, 'dp')
- attend_scale_grad: float32 [2, 1024], P(None, 'dp')
- second_gain_grad: float32 [2, 1024], P(None, 'dp')
- second_shift_grad: float32 [2, 1024], P(None, 'dp')
- up_weight_grad: float32 [2, 1024, 4096], P(None, 'dp', 'mp')
- up_bias_grad: float32 [2, 4096], P(None, ('mp', 'dp'))
- down_weight_grad: float32 [2, 1024, 4096], P(None, 'dp', 'mp')
- down_bias_grad: float32 [2, 1024], P(None, 'dp')
- feed_scale_grad: float32 [2, 1024], P(None, 'dp')
The draws below stay inside these ranges and needn't reach their ends.
Inputs may be any that keep to these rules, and one draw needn't show every extreme that they name: `segments`: in every row the 197 slots of segment 0 form one run, the 50 slots of segment 1 form another, and every other slot holds 2.
All inputs are finite; a program needn't handle non-finite values.
Results may differ from the reference program's by a relative error of at most 0.025.
Values may be sent and summed in bfloat16 or wider, within the bound.
No kernel may reach another device: no remote copies, remote signals or barrier semaphores. Data moves between devices by JAX's collectives and lax.ppermute only.
A program may use at most 192 MiB of HBM per device.

```python
import math
import jax
import jax.numpy as jnp
from jax import lax

D = 1024
HEADS = 16
HD = 64
FF = 4096
SLOTS = 256
CROP_A = 197
CROP_B = 50
LAYERS = 2
ROWS = 32
N_MP = 4


def draw_segments(key, part):
    key = jax.random.fold_in(key, 7)
    keys = jax.random.split(key, 3)
    spare = SLOTS - CROP_A - CROP_B
    order = jax.random.randint(keys[0], (ROWS, 1), 0, 2).astype(jnp.int32)
    before = jax.random.randint(keys[1], (ROWS, 1), 0, spare + 1).astype(jnp.int32)
    between = jax.random.randint(keys[2], (ROWS, 1), 0, spare + 1 - before).astype(jnp.int32)
    first_length = jnp.where(order == 0, CROP_A, CROP_B).astype(jnp.int32)
    second_length = (CROP_A + CROP_B - first_length).astype(jnp.int32)
    second_start = before + first_length + between
    slot = jnp.arange(SLOTS, dtype=jnp.int32)[None, :]
    labels = jnp.full((ROWS, SLOTS), 2, dtype=jnp.int32)
    labels = jnp.where((slot >= before) & (slot < before + first_length), order, labels)
    labels = jnp.where((slot >= second_start) & (slot < second_start + second_length), 1 - order, labels)
    return labels.astype(jnp.int32)


def raised(array, key, source, target, shards_of, factor):
    owner, partner = [(jnp.arange(array.shape[position]) // (array.shape[position] // shards_of)).reshape([-1 if axis == position else 1 for axis in range(array.ndim)]) for position in (source, target)]
    chosen = jax.random.permutation(key, shards_of)[partner]
    strong = (owner == chosen) | (owner == (partner + shards_of // 2) % shards_of)
    return jnp.where(strong, factor * array, array)


def levels(rng, dims, cuts, least, largest):
    def one(axis_at, shards_of):
        draws = jax.random.uniform(jax.random.fold_in(jax.random.fold_in(rng, 6), axis_at), (shards_of,), jnp.float32, least / len(cuts), largest / len(cuts))
        return jnp.repeat(jnp.exp(draws), dims[axis_at] // shards_of).reshape((-1,) + (1,) * (len(dims) - axis_at - 1))

    factor_of = one(*cuts[0])
    for cut in cuts[1:]:
        factor_of = factor_of * one(*cut)
    return factor_of


def centred(own_key, extent, deviation, most, pieces=(), kind=jnp.bfloat16):
    values = deviation * jax.random.normal(own_key, extent, jnp.float32)
    if pieces:
        values = values * levels(own_key, extent, pieces, -0.22, 0.18)
    return jnp.clip(values, -most, most).astype(kind)


def noise_with(own_key, dims, scale, most, pieces, heavy, kind=jnp.bfloat16):
    entries = scale * jax.random.normal(own_key, dims, jnp.float32)
    if pieces:
        entries = entries * levels(own_key, dims, pieces, -0.22, 0.18)
    return jnp.clip(raised(entries, jax.random.fold_in(own_key, 3), *heavy), -most, most).astype(kind)


def setup_inputs(seed: int = 0) -> dict:
    key_of = jax.random.split(jax.random.key(seed), 21)
    activations = centred(key_of[0], (ROWS, SLOTS, D), 1.0, 6.0, ((0, 8),))
    segments = draw_segments(jax.random.fold_in(key_of[20], 71), 0)
    first_gain = jnp.clip(1.0 + 0.1 * jax.random.normal(key_of[2], (LAYERS, D), jnp.float32), 0.5, 1.5)
    first_shift = centred(key_of[3], (LAYERS, D), 0.3, 1.5, (), jnp.float32)
    query_weight = centred(key_of[4], (LAYERS, D, D), D ** -0.5, 0.1875, ((2, 4),))
    key_weight = centred(key_of[5], (LAYERS, D, D), D ** -0.5, 0.1875, ((2, 4),))
    value_weight = centred(key_of[6], (LAYERS, D, D), D ** -0.5, 0.1875, ((2, 4),))
    query_bias = centred(key_of[7], (LAYERS, D), 0.5, 3.0, ((1, 4),), jnp.float32)
    value_bias = centred(key_of[8], (LAYERS, D), 0.5, 3.0, ((1, 4),), jnp.float32)
    out_weight = centred(key_of[9], (LAYERS, D, D), (D // 16) ** -0.5, 0.75, ((2, 4),))
    out_bias = centred(key_of[10], (LAYERS, D), 0.3, 1.5, (), jnp.float32)
    attend_scale = jnp.clip(1.0 + 0.15 * jax.random.normal(key_of[11], (LAYERS, D), jnp.float32), 0.25, 1.75)
    second_gain = jnp.clip(1.0 + 0.1 * jax.random.normal(key_of[12], (LAYERS, D), jnp.float32), 0.5, 1.5)
    second_shift = centred(key_of[13], (LAYERS, D), 0.3, 1.5, (), jnp.float32)
    up_weight = centred(key_of[14], (LAYERS, D, FF), D ** -0.5, 0.1875, ((2, 4),))
    up_bias = centred(key_of[15], (LAYERS, FF), 0.3, 1.5, ((1, 4),), jnp.float32)
    down_weight = centred(key_of[16], (LAYERS, D, FF), (FF // 4) ** -0.5, 0.1875, ((2, 4),))
    down_bias = centred(key_of[17], (LAYERS, D), 0.3, 1.5, (), jnp.float32)
    feed_scale = jnp.clip(1.0 + 0.15 * jax.random.normal(key_of[18], (LAYERS, D), jnp.float32), 0.25, 1.75)
    cotangent = noise_with(key_of[19], (ROWS, SLOTS, D), 1.0, 6.0, ((0, 8),), (0, 2, 8, 2.0))
    return dict(activations=activations, segments=segments, first_gain=first_gain, first_shift=first_shift, query_weight=query_weight, key_weight=key_weight, value_weight=value_weight, query_bias=query_bias, value_bias=value_bias, out_weight=out_weight, out_bias=out_bias, attend_scale=attend_scale, second_gain=second_gain, second_shift=second_shift, up_weight=up_weight, up_bias=up_bias, down_weight=down_weight, down_bias=down_bias, feed_scale=feed_scale, cotangent=cotangent)


@jax.custom_vjp
def low(v):
    return lax.optimization_barrier(v.astype(jnp.bfloat16)).astype(jnp.float32)

@jax.custom_vjp
def low_back(v):
    return v

def low_keep(v):
    return (low(v), None)

def low_pass(kept, grad):
    return (grad,)

def back_keep(v):
    return (v, None)

def back_low(kept, grad):
    return (low(grad),)
low.defvjp(low_keep, low_pass)
low_back.defvjp(back_keep, back_low)
EPSILON = 1e-06
HIGHEST = lax.Precision.HIGHEST

def norm_rows(values, gain, shift):
    center = values - lax.optimization_barrier(jnp.mean(values, axis=-1, keepdims=True))
    spread = lax.optimization_barrier(jnp.mean(center * center, axis=-1, keepdims=True))
    return center * lax.rsqrt(spread + EPSILON) * gain + shift

def project(values, weight):
    return jnp.einsum('rsk,kn->rsn', values, weight, precision=HIGHEST)

def project_back(values, weight):
    return jnp.einsum('rsk,nk->rsn', values, weight, precision=HIGHEST)

def one_layer(current, layer_params, same_crop):
    first_gain, first_shift, query_weight, key_weight, value_weight, query_bias, value_bias, out_weight, out_bias, attend_scale, second_gain, second_shift, up_weight, up_bias, down_weight, down_bias, feed_scale = layer_params
    rows, slots = (current.shape[0], current.shape[1])
    group = D // N_MP
    hidden_group = FF // N_MP
    heads_group = HEADS // N_MP
    shape_heads = (rows, slots, heads_group, HD)
    normed = low(norm_rows(current, first_gain, first_shift))
    attended = jnp.zeros_like(current)
    for index in range(N_MP):
        cols = slice(index * group, (index + 1) * group)
        mine = low_back(normed)
        query = low(low_back(project(mine, query_weight[:, cols]) + query_bias[cols]))
        key = low(low_back(project(mine, key_weight[:, cols])))
        value = low(low_back(project(mine, value_weight[:, cols]) + value_bias[cols]))
        scores = jnp.einsum('rqhd,rkhd->rhqk', query.reshape(shape_heads), key.reshape(shape_heads), precision=HIGHEST) * HD ** (-0.5)
        scores = jnp.where(same_crop, low_back(scores), -1e+30)
        probs = low(jax.nn.softmax(scores, axis=-1))
        mixed = jnp.einsum('rhqk,rkhd->rqhd', probs, value.reshape(shape_heads), precision=HIGHEST)
        mixed = low(low_back(mixed.reshape(rows, slots, group)))
        attended = attended + low(project_back(mixed, out_weight[:, cols]))
    middle = current + attend_scale * (low_back(attended) + out_bias)
    normed2 = low(norm_rows(middle, second_gain, second_shift))
    fed = jnp.zeros_like(current)
    for index in range(N_MP):
        cols = slice(index * hidden_group, (index + 1) * hidden_group)
        mine = low_back(normed2)
        before_gelu = low_back(project(mine, up_weight[:, cols]) + up_bias[cols])
        activated = low(jax.nn.gelu(before_gelu, approximate=False))
        fed = fed + low(project_back(activated, down_weight[:, cols]))
    return middle + feed_scale * (low_back(fed) + down_bias)

def all_layers(current, params, segment_block):
    same_crop = (segment_block[:, :, None] == segment_block[:, None, :])[:, None]
    for layer in range(LAYERS):
        current = one_layer(current, tuple((p[layer] for p in params)), same_crop)
    return current

def reference(activations, segments, first_gain, first_shift, query_weight, key_weight, value_weight, query_bias, value_bias, out_weight, out_bias, attend_scale, second_gain, second_shift, up_weight, up_bias, down_weight, down_bias, feed_scale, cotangent):
    params = tuple((p.astype(jnp.float32) for p in (first_gain, first_shift, query_weight, key_weight, value_weight, query_bias, value_bias, out_weight, out_bias, attend_scale, second_gain, second_shift, up_weight, up_bias, down_weight, down_bias, feed_scale)))
    block_rows = math.gcd(ROWS, 16)
    blocks = ROWS // block_rows

    def block_step(carry, index):
        start = (index * block_rows).astype(jnp.int32)
        inputs = lax.dynamic_slice_in_dim(activations, start, block_rows, 0).astype(jnp.float32)
        segment_block = lax.dynamic_slice_in_dim(segments, start, block_rows, 0)
        seed_grad = lax.dynamic_slice_in_dim(cotangent, start, block_rows, 0).astype(jnp.float32)

        def forward(values, weights):
            return all_layers(values, weights, segment_block)
        output, pullback = jax.vjp(forward, inputs, params)
        input_part, param_part = pullback(seed_grad)
        carry = jax.tree.map(jnp.add, carry, param_part)
        return (carry, (output.astype(jnp.bfloat16), input_part))
    zeros = tuple((jnp.zeros_like(p) for p in params))
    grads, (outputs, input_parts) = lax.scan(block_step, zeros, jnp.arange(blocks).astype(jnp.int32))
    result = outputs.reshape(ROWS, SLOTS, D)
    input_grad = input_parts.reshape(ROWS, SLOTS, D)
    return (result, input_grad, grads[0], grads[1], grads[2], grads[3], grads[4], grads[5], grads[6], grads[7], grads[8], grads[9], grads[10], grads[11], grads[12], grads[13], grads[14], grads[15], grads[16])
```

```python
import functools
import math

import jax
import jax.numpy as jnp
from jax import lax
from jax.experimental import pallas as pl
from jax.experimental.pallas import tpu as pltpu
from jax.sharding import PartitionSpec as P

HD = 64
EPSILON = 1e-06
MASKED = -1e30
F32 = jnp.float32
BF16 = jnp.bfloat16
CONTRACT_LAST = (((1,), (1,)), ((), ()))
CONTRACT_ROWS = (((0,), (0,)), ((), ()))
VMEM_LIMIT = 56 * 1024 * 1024
SAMPLE = 2


def dot(a, b):
    return jnp.dot(a, b, preferred_element_type=F32)


def dot_last(a, b):
    return lax.dot_general(a, b, CONTRACT_LAST, preferred_element_type=F32)


def dot_rows(a, b):
    return lax.dot_general(a, b, CONTRACT_ROWS, preferred_element_type=F32)


def normalise(values):
    center = values - jnp.mean(values, axis=-1, keepdims=True)
    spread = jnp.mean(center * center, axis=-1, keepdims=True)
    factor = lax.rsqrt(spread + EPSILON)
    return center * factor, factor


def norm_back(hat, factor, gain, grad):
    inner = grad * gain
    first = jnp.mean(inner, axis=-1, keepdims=True)
    second = jnp.mean(inner * hat, axis=-1, keepdims=True)
    return factor * (inner - first - hat * second)


def column_sum(values):
    return jnp.sum(values, axis=0, keepdims=True)


def fetch(plan, sems):
    copies = []
    for index, (source, target) in enumerate(plan):
        copy = pltpu.make_async_copy(source, target, sems.at[index])
        copy.start()
        copies.append(copy)
    return copies


def residual(values, scale, mine, theirs, bias):
    return values + scale * (mine.astype(F32) + theirs.astype(F32) + bias)


def attend_forward(layer, *refs):
    if layer == 0:
        source, refs = refs[0], refs[1:]
    else:
        (middle, mine, theirs, feed_scale, down_bias), refs = refs[:5], refs[5:]
    (mask, gain, shift, query_bias, value_bias) = refs[:5]
    (wq0, wq1, wk0, wk1, wv0, wv1, wo0, wo1) = refs[5:13]
    (current, normed_out, query_out, key_out, value_out, probs_out, mixed_out, part) = refs[13:21]
    wq, wk, wv, wo, sems = refs[21:]
    half = wq0.shape[2]
    now = slice(layer, layer + 1)
    plan = []
    for own, other, target in ((wq0, wq1, wq), (wk0, wk1, wk), (wv0, wv1, wv), (wo0, wo1, wo)):
        plan.append((own.at[layer], target.at[:, :half]))
        plan.append((other.at[layer], target.at[:, half:]))
    copies = fetch(plan, sems)
    if layer == 0:
        values = source[...].astype(F32)
    else:
        before = slice(layer - 1, layer)
        values = residual(
            middle[...], feed_scale[before], mine[...], theirs[...], down_bias[before]
        )
    current[...] = values
    hat, _ = normalise(values)
    normed = (hat * gain[now] + shift[now]).astype(BF16)
    normed_out[...] = normed
    copies[0].wait()
    copies[1].wait()
    query_out[...] = (dot(normed, wq[...]) + query_bias[now]).astype(BF16)
    copies[2].wait()
    copies[3].wait()
    key_out[...] = dot(normed, wk[...]).astype(BF16)
    copies[4].wait()
    copies[5].wait()
    value_out[...] = (dot(normed, wv[...]) + value_bias[now]).astype(BF16)
    pairs = 2 * half // (2 * HD)
    lane = lax.broadcasted_iota(jnp.int32, (values.shape[0], 2 * HD), 1)
    scale = jnp.asarray(HD ** (-0.5), BF16)
    blocked = mask[...]
    for pair in range(pairs):
        cols = slice(pair * 2 * HD, (pair + 1) * 2 * HD)
        query = query_out[:, cols] * scale
        key = key_out[:, cols]
        value = value_out[:, cols]
        mixed = []
        for side in range(2):
            lanes = (lane < HD) if side == 0 else (lane >= HD)
            scores = dot_last(jnp.where(lanes, query, jnp.zeros_like(query)), key) + blocked
            top = jnp.max(scores, axis=-1, keepdims=True)
            weights = jnp.exp(scores - top)
            total = jnp.sum(weights, axis=-1, keepdims=True)
            probs = (weights * (1.0 / total)).astype(BF16)
            probs_out[2 * pair + side] = probs
            mixed.append(dot(probs, value))
        mixed_out[:, cols] = jnp.where(lane < HD, mixed[0], mixed[1]).astype(BF16)
    copies[6].wait()
    copies[7].wait()
    part[...] = dot_last(mixed_out[...], wo[...]).astype(BF16)


def feed_forward(layer, *refs):
    (current, mine, theirs, attend_scale, out_bias, gain, shift, up_bias) = refs[:8]
    (wu0, wu1, wd0, wd1) = refs[8:12]
    (middle, normed_out, act0, act1, slope0, slope1, part) = refs[12:19]
    wu, wd, sems = refs[19:]
    half = wu0.shape[2]
    width = half // 2
    now = slice(layer, layer + 1)
    plan = []
    for index in range(4):
        cols = slice((index % 2) * width, (index % 2 + 1) * width)
        plan.append(((wu0, wu1)[index // 2].at[layer, :, cols], wu.at[index]))
    for index in range(4):
        cols = slice((index % 2) * width, (index % 2 + 1) * width)
        plan.append(((wd0, wd1)[index // 2].at[layer, :, cols], wd.at[index]))
    copies = fetch(plan, sems)
    values = residual(current[...], attend_scale[now], mine[...], theirs[...], out_bias[now])
    middle[...] = values
    hat, _ = normalise(values)
    normed = (hat * gain[now] + shift[now]).astype(BF16)
    normed_out[...] = normed
    total = None
    for index in range(4):
        copies[index].wait()
        before = dot(normed, wu[index]) + up_bias[now, index * width : (index + 1) * width]
        lower = 0.5 * (1.0 + lax.erf(before * math.sqrt(0.5)))
        active = (before * lower).astype(BF16)
        bell = jnp.exp(-0.5 * before * before) * (1.0 / math.sqrt(2.0 * math.pi))
        slope = (lower + before * bell).astype(BF16)
        cols = slice((index % 2) * width, (index % 2 + 1) * width)
        (act0, act1)[index // 2][:, cols] = active
        (slope0, slope1)[index // 2][:, cols] = slope
        copies[4 + index].wait()
        term = dot_last(active, wd[index])
        total = term if total is None else total + term
    part[...] = total.astype(BF16)


def finish_forward(layer, middle, mine, theirs, feed_scale, down_bias, result):
    now = slice(layer, layer + 1)
    result[...] = residual(
        middle[...], feed_scale[now], mine[...], theirs[...], down_bias[now]
    ).astype(BF16)


def feed_backward(layer, last, *refs):
    if last:
        source, refs = refs[0], refs[1:]
    else:
        (after, deep, deep_mine, deep_theirs, deep_gain), refs = refs[:5], refs[5:]
    (fed_mine, fed_theirs, feed_scale, down_bias, slope0, slope1) = refs[:6]
    (wu0, wu1, wd0, wd1) = refs[6:10]
    (grad_out, grad_fed_out, before0, before1, part, sums, wide_sums) = refs[10:17]
    wu, wd, sems = refs[17:]
    half = wu0.shape[2]
    width = half // 2
    now = slice(layer, layer + 1)
    plan = []
    for index in range(4):
        cols = slice((index % 2) * width, (index % 2 + 1) * width)
        plan.append(((wd0, wd1)[index // 2].at[layer, :, cols], wd.at[index]))
    for index in range(4):
        cols = slice((index % 2) * width, (index % 2 + 1) * width)
        plan.append(((wu0, wu1)[index // 2].at[layer, :, cols], wu.at[index]))
    copies = fetch(plan, sems)
    if last:
        grad = source[...].astype(F32)
        zero = jnp.zeros((1, grad.shape[1]), F32)
        sums[2:3] = zero
        sums[3:4] = zero
    else:
        hat, factor = normalise(deep[...])
        grad_normed = deep_mine[...].astype(F32) + deep_theirs[...].astype(F32)
        grad = after[...] + norm_back(hat, factor, deep_gain[layer + 1 : layer + 2], grad_normed)
        sums[2:3] = column_sum(grad_normed * hat)
        sums[3:4] = column_sum(grad_normed)
    grad_out[...] = grad
    scaled = feed_scale[now] * grad
    grad_fed = scaled.astype(BF16)
    grad_fed_out[...] = grad_fed
    sums[0:1] = column_sum(scaled)
    fed = fed_mine[...].astype(F32) + fed_theirs[...].astype(F32)
    sums[1:2] = column_sum(grad * (fed + down_bias[now]))
    total = None
    for index in range(4):
        cols = slice((index % 2) * width, (index % 2 + 1) * width)
        copies[index].wait()
        grad_active = dot(grad_fed, wd[index])
        slope = (slope0, slope1)[index // 2][:, cols].astype(F32)
        before = (grad_active * slope).astype(BF16)
        (before0, before1)[index // 2][:, cols] = before
        wide_sums[:, index * width : (index + 1) * width] = column_sum(before.astype(F32))
        copies[4 + index].wait()
        term = dot_last(before, wu[index])
        total = term if total is None else total + term
    part[...] = total.astype(BF16)


def attend_backward(layer, *refs):
    (grad_in, middle, mine, theirs, gain) = refs[:5]
    (att_mine, att_theirs, attend_scale, out_bias) = refs[5:9]
    (query_in, key_in, value_in, probs_in) = refs[9:13]
    (wq0, wq1, wk0, wk1, wv0, wv1, wo0, wo1) = refs[13:21]
    (grad_out, grad_att_out, gq, gk, gv, part, sums, wide_sums) = refs[21:29]
    wq, wk, wv, wo, mixed_scratch, sems = refs[29:]
    half = wq0.shape[2]
    now = slice(layer, layer + 1)
    plan = []
    for own, other, target in ((wo0, wo1, wo), (wq0, wq1, wq), (wk0, wk1, wk), (wv0, wv1, wv)):
        plan.append((own.at[layer], target.at[:, :half]))
        plan.append((other.at[layer], target.at[:, half:]))
    copies = fetch(plan, sems)
    hat, factor = normalise(middle[...])
    grad_normed = mine[...].astype(F32) + theirs[...].astype(F32)
    grad = grad_in[...] + norm_back(hat, factor, gain[now], grad_normed)
    grad_out[...] = grad
    scaled = attend_scale[now] * grad
    grad_att = scaled.astype(BF16)
    grad_att_out[...] = grad_att
    sums[0:1] = column_sum(scaled)
    attended = att_mine[...].astype(F32) + att_theirs[...].astype(F32)
    sums[1:2] = column_sum(grad * (attended + out_bias[now]))
    sums[2:3] = column_sum(grad_normed * hat)
    sums[3:4] = column_sum(grad_normed)
    copies[0].wait()
    copies[1].wait()
    mixed_scratch[...] = dot(grad_att, wo[...]).astype(BF16)
    pairs = 2 * half // (2 * HD)
    lane = lax.broadcasted_iota(jnp.int32, (grad.shape[0], 2 * HD), 1)
    scale = HD ** (-0.5)
    for pair in range(pairs):
        cols = slice(pair * 2 * HD, (pair + 1) * 2 * HD)
        query = query_in[:, cols]
        key = key_in[:, cols]
        value = value_in[:, cols]
        mixed = mixed_scratch[:, cols]
        found = []
        for side in range(2):
            lanes = (lane < HD) if side == 0 else (lane >= HD)
            probs_low = probs_in[2 * pair + side]
            probs = probs_low.astype(F32)
            grad_probs = dot_last(jnp.where(lanes, mixed, jnp.zeros_like(mixed)), value)
            weighted = probs * grad_probs
            row = jnp.sum(weighted, axis=-1, keepdims=True)
            grad_scores = (weighted - probs * row).astype(BF16)
            found.append(
                (dot(grad_scores, key), dot_rows(grad_scores, query), dot_rows(probs_low, mixed))
            )
        first = lane < HD
        gq[:, cols] = (jnp.where(first, found[0][0], found[1][0]) * scale).astype(BF16)
        gk[:, cols] = (jnp.where(first, found[0][1], found[1][1]) * scale).astype(BF16)
        gv[:, cols] = jnp.where(first, found[0][2], found[1][2]).astype(BF16)
    wide_sums[0:1] = column_sum(gq[...].astype(F32))
    wide_sums[1:2] = column_sum(gv[...].astype(F32))
    for copy in copies[2:]:
        copy.wait()
    total = dot_last(gq[...], wq[...]) + dot_last(gk[...], wk[...]) + dot_last(gv[...], wv[...])
    part[...] = total.astype(BF16)


def finish_backward(after, deep, mine, theirs, gain, grad_out, sums):
    hat, factor = normalise(deep[...])
    grad_normed = mine[...].astype(F32) + theirs[...].astype(F32)
    grad_out[...] = after[...] + norm_back(hat, factor, gain[0:1], grad_normed)
    sums[0:1] = column_sum(grad_normed * hat)
    sums[1:2] = column_sum(grad_normed)


def weight_grad(chunks, count, has_other, places, *refs):
    lefts = refs[: 2 * count]
    rights = refs[2 * count : 4 * count]
    refs = refs[4 * count :]
    if has_other:
        others, refs = refs[:count], refs[count:]
    outs, turned = refs[:count], refs[count:]
    step = pl.program_id(0)
    tokens = lefts[0].shape[0]

    @pl.when(step == 0)
    def _():
        for index in range(count):
            for sample in range(2):
                turned[index][:, sample * tokens : (sample + 1) * tokens] = lefts[
                    2 * index + sample
                ][...].T

    for index in range(count):
        right = jnp.concatenate([rights[2 * index][...], rights[2 * index + 1][...]], axis=0)
        product = dot(turned[index][...], right)
        rows = product.shape[0] // chunks
        for chunk in range(chunks):
            at = pl.multiple_of(places[index, chunk] * rows, rows)
            block = product[chunk * rows : (chunk + 1) * rows]
            if has_other:
                block = block + others[index][pl.ds(at, rows), :].astype(F32)
            outs[index][pl.ds(at, rows), :] = block.astype(BF16)


def whole(array):
    rank = len(array.shape)
    return pl.BlockSpec(array.shape, lambda i, rank=rank: (0,) * rank)


def one_of(array, index):
    rank = len(array.shape)
    return pl.BlockSpec(
        (None,) + array.shape[1:], lambda i, index=index, rank=rank: (index,) + (0,) * (rank - 1)
    )


ANYWHERE = pl.BlockSpec(memory_space=pl.ANY)


def run(body, inputs, specs, outputs, scratch, name, flops):
    shapes = [jax.ShapeDtypeStruct(shape, kind) for shape, kind in outputs]
    moved = sum(math.prod(shape) * jnp.dtype(kind).itemsize for shape, kind in outputs)
    moved += sum(
        math.prod(value.shape) * value.dtype.itemsize // value.shape[0]
        for value in inputs
    )
    return pl.pallas_call(
        body,
        out_shape=shapes,
        grid=(1,),
        in_specs=specs,
        out_specs=[whole(shape) for shape in shapes],
        scratch_shapes=scratch,
        compiler_params=pltpu.CompilerParams(vmem_limit_bytes=VMEM_LIMIT),
        cost_estimate=pl.CostEstimate(flops=flops, bytes_accessed=moved, transcendentals=0),
        name=name,
    )(*inputs)


def weight_grads(pairs, places, others, blocks, name):
    count = len(pairs)
    inputs, specs = [], []
    for lefts, _ in pairs:
        for left in lefts:
            inputs.append(left)
            specs.append(pl.BlockSpec(left.shape, lambda j, table: (0, 0)))
    for _, rights in pairs:
        for right, start in rights:
            width = WIDTHS(right, start) // blocks
            inputs.append(right)
            first = start[0] // width
            specs.append(
                pl.BlockSpec((right.shape[0], width), lambda j, table, first=first: (0, first + j))
            )
    shapes, out_specs, scratch = [], [], []
    for lefts, rights in pairs:
        width = WIDTHS(*rights[0])
        rows = lefts[0].shape[1]
        shapes.append(jax.ShapeDtypeStruct((rows, width), BF16))
        out_specs.append(pl.BlockSpec((rows, width // blocks), lambda j, table: (0, j)))
        scratch.append(pltpu.VMEM((rows, 2 * lefts[0].shape[0]), BF16))
    if others is not None:
        for other, spec in zip(others, out_specs):
            inputs.append(other)
            specs.append(spec)
    tokens = 2 * pairs[0][0][0].shape[0]
    flops = sum(2 * tokens * math.prod(shape.shape) for shape in shapes)
    moved = sum(2 * math.prod(shape.shape) for shape in shapes) * (1 if others is None else 2)
    moved += sum(value.size * 2 for value in inputs[: 4 * count])
    return pl.pallas_call(
        functools.partial(weight_grad, places.shape[1], count, others is not None),
        out_shape=shapes,
        grid_spec=pltpu.PrefetchScalarGridSpec(
            num_scalar_prefetch=1,
            grid=(blocks,),
            in_specs=specs,
            out_specs=out_specs,
            scratch_shapes=scratch,
        ),
        compiler_params=pltpu.CompilerParams(vmem_limit_bytes=VMEM_LIMIT),
        cost_estimate=pl.CostEstimate(flops=flops, bytes_accessed=moved, transcendentals=0),
        name=name,
    )(places, *inputs)


def WIDTHS(right, span):
    return span[1] - span[0]


def ring_order(n):
    return list(range(0, n, 2)) + list(range(n - 1, 0, -2))


def ring_scatter(clockwise, counter, n):
    order = ring_order(n)
    forward = [(order[i], order[(i + 1) % n]) for i in range(n)]
    backward = [(b, a) for a, b in forward]
    rows = clockwise.shape[0] // n
    one, two = clockwise[:rows], counter[:rows]
    for step in range(n - 1):
        one = lax.ppermute(one, "dp", forward)
        two = lax.ppermute(two, "dp", backward)
        span = slice((step + 1) * rows, (step + 2) * rows)
        one = one.astype(F32) + clockwise[span].astype(F32)
        two = two.astype(F32) + counter[span].astype(F32)
        if step < n - 2:
            one, two = one.astype(BF16), two.astype(BF16)
    return one, two


def small_scatter(packed, n):
    me = lax.axis_index("dp")
    turned = jnp.take(packed, (me + jnp.arange(n)) % n, axis=0)
    total = turned[0]
    for shift in range(1, n):
        total = total + lax.ppermute(
            turned[shift], "dp", [(i, (i + shift) % n) for i in range(n)]
        )
    return total


def per_device(
    n,
    activations,
    segments,
    first_gain,
    first_shift,
    query_weight,
    key_weight,
    value_weight,
    query_bias,
    value_bias,
    out_weight,
    out_bias,
    attend_scale,
    second_gain,
    second_shift,
    up_weight,
    up_bias,
    down_weight,
    down_bias,
    feed_scale,
    cotangent,
):
    rows, slots, width = activations.shape
    layers = first_gain.shape[0]
    mp = lax.axis_index("mp")
    core = mp % 2
    mine_rows = rows // 2
    tokens = mine_rows // SAMPLE * slots
    heads_half = query_weight.shape[2]
    hidden_half = up_weight.shape[2]
    features = 2 * heads_half
    hidden = 2 * hidden_half
    heads = features // HD
    samples = range(SAMPLE)
    ring = n <= 8 and n % 2 == 0

    def swap_core(value):
        return lax.ppermute(value, "mp", [(i, i ^ 1) for i in range(4)])

    def swap_x(value):
        return lax.ppermute(value, "mp", [(i, i ^ 2) for i in range(4)])

    biases = jnp.concatenate([query_bias, value_bias, up_bias], axis=1)
    wq1, wk1, wv1 = swap_core(query_weight), swap_core(key_weight), swap_core(value_weight)
    biases_other = swap_core(biases)
    wo1 = swap_core(out_weight)
    wu1, wd1 = swap_core(up_weight), swap_core(down_weight)
    both = jnp.concatenate([biases, biases_other], axis=1)
    span = heads_half * 2 + hidden_half
    query_bias_all = jnp.concatenate([both[:, :heads_half], both[:, span : span + heads_half]], 1)
    value_bias_all = jnp.concatenate(
        [both[:, heads_half:features], both[:, span + heads_half : span + features]], 1
    )
    up_bias_all = jnp.concatenate([both[:, features:span], both[:, span + features :]], 1)
    attend_weights = [query_weight, wq1, key_weight, wk1, value_weight, wv1, out_weight, wo1]
    feed_weights = [up_weight, wu1, down_weight, wd1]

    def own_rows(value):
        start = (core * mine_rows,) + (0,) * (value.ndim - 1)
        return lax.dynamic_slice(value, start, (mine_rows,) + value.shape[1:])

    own_segments = own_rows(segments)
    same = own_segments[:, :, None] == own_segments[:, None, :]
    masks = jnp.where(same, 0.0, MASKED).astype(F32)
    own_input = own_rows(activations)
    own_cotangent = own_rows(cotangent)
    assert tokens == slots

    attend_scratch = [
        pltpu.VMEM((width, features), BF16),
        pltpu.VMEM((width, features), BF16),
        pltpu.VMEM((width, features), BF16),
        pltpu.VMEM((width, features), BF16),
    ]
    feed_scratch = [
        pltpu.VMEM((4, width, hidden_half // 2), BF16),
        pltpu.VMEM((4, width, hidden_half // 2), BF16),
        pltpu.SemaphoreType.DMA((8,)),
    ]
    act = ((tokens, width), BF16)
    state = ((tokens, width), F32)
    head = ((tokens, features), BF16)
    hid = ((tokens, hidden_half), BF16)
    probs_shape = ((heads, slots, slots), BF16)
    attend_flops = 2 * tokens * width * features * 4 + 4 * tokens * slots * heads * 128
    feed_flops = 4 * tokens * width * hidden

    saved = [[None] * SAMPLE for _ in range(layers)]
    state_now = [None] * SAMPLE
    fed = [None] * SAMPLE
    for layer in range(layers):
        parts = []
        for m in samples:
            if layer == 0:
                inputs, specs = [own_input], [one_of(own_input, m)]
            else:
                inputs = [state_now[m], fed[m][0], fed[m][1], feed_scale, down_bias]
                specs = [whole(v) for v in inputs]
                inputs[3:5] = [feed_scale, down_bias]
            more = [first_gain, first_shift, query_bias_all, value_bias_all]
            inputs = inputs + [masks] + more + attend_weights
            specs = specs + [one_of(masks, m)] + [whole(v) for v in more] + [ANYWHERE] * 8
            outs = run(
                functools.partial(attend_forward, layer),
                inputs,
                specs,
                [state, act, head, head, head, probs_shape, head, act],
                attend_scratch + [pltpu.SemaphoreType.DMA((8,))],
                "attend_forward",
                attend_flops,
            )
            kept = dict(zip(("current", "normed", "q", "k", "v", "probs", "mixed"), outs))
            saved[layer][m] = kept
            kept["att"] = (outs[7], swap_x(outs[7]))
        for m in samples:
            kept = saved[layer][m]
            vectors = [attend_scale, out_bias, second_gain, second_shift, up_bias_all]
            inputs = [kept["current"], *kept["att"]] + vectors
            outs = run(
                functools.partial(feed_forward, layer),
                inputs + feed_weights,
                [whole(v) for v in inputs] + [ANYWHERE] * 4,
                [state, act, hid, hid, hid, hid, act],
                feed_scratch,
                "feed_forward",
                feed_flops,
            )
            kept.update(zip(("middle", "normed2", "act0", "act1", "slope0", "slope1"), outs))
            state_now[m] = outs[0]
            fed[m] = kept["fed"] = (outs[6], swap_x(outs[6]))

    results = []
    for m in samples:
        inputs = [state_now[m], *fed[m], feed_scale, down_bias]
        results.append(
            run(
                functools.partial(finish_forward, layers - 1),
                inputs,
                [whole(v) for v in inputs],
                [act],
                [],
                "finish_forward",
                tokens * width,
            )[0]
        )

    if ring:
        me = lax.axis_index("dp")
        place = jnp.where(me % 2 == 0, me // 2, (2 * n - 1 - me) // 2)
        chunk = jnp.arange(n)
        chunk_place = jnp.where(chunk % 2 == 0, chunk // 2, (2 * n - 1 - chunk) // 2)
        table_one = (place - 1 - chunk_place) % n
        table_two = (chunk_place - place - 1) % n
    else:
        table_one = table_two = jnp.arange(8)
    places_feed = jnp.stack([table_one, table_two]).astype(jnp.int32)
    places_attend = jnp.stack([table_one, table_one, table_two, table_two]).astype(jnp.int32)

    def reduce_pair(one, two):
        if ring:
            return ring_scatter(one, two, n)
        both_now = jnp.concatenate([one, two], axis=1).astype(F32)
        done = lax.psum_scatter(both_now, "dp", scatter_dimension=0, tiled=True)
        return done[:, : one.shape[1]], done[:, one.shape[1] :]

    grads = [None] * layers
    smalls = [None] * layers
    late_sums = [None] * layers
    carry = [None] * SAMPLE
    for layer in reversed(range(layers)):
        last = layer == layers - 1
        feed_sums, attend_sums = [], []
        for m in samples:
            kept = saved[layer][m]
            if last:
                inputs, specs = [own_cotangent], [one_of(own_cotangent, m)]
            else:
                inputs = [*carry[m], first_gain]
                specs = [whole(v) for v in inputs]
            more = [*kept["fed"], feed_scale, down_bias, kept["slope0"], kept["slope1"]]
            outs = run(
                functools.partial(feed_backward, layer, last),
                inputs + more + feed_weights,
                specs + [whole(v) for v in more] + [ANYWHERE] * 4,
                [state, act, hid, hid, act, ((4, width), F32), ((1, hidden), F32)],
                feed_scratch,
                "feed_backward",
                feed_flops,
            )
            kept.update(zip(("grad", "grad_fed", "before0", "before1"), outs))
            kept["n2"] = (outs[4], swap_x(outs[4]))
            feed_sums.append(outs[5:])
        kept = saved[layer]

        def spans(name, length, offset=0):
            return [(kept[m][name], (offset, offset + length)) for m in samples]

        lefts_up = [kept[m]["normed2"] for m in samples]
        lefts_down = [kept[m]["grad_fed"] for m in samples]
        given = weight_grads(
            [(lefts_up, spans("before1", hidden_half)), (lefts_down, spans("act1", hidden_half))],
            places_feed,
            None,
            4,
            "feed_grads_given",
        )
        taken = [swap_core(value) for value in given]
        up_part, down_part = weight_grads(
            [(lefts_up, spans("before0", hidden_half)), (lefts_down, spans("act0", hidden_half))],
            places_feed,
            taken,
            4,
            "feed_grads",
        )
        up_grad, down_grad = reduce_pair(up_part, down_part)
        for m in samples:
            own = kept[m]
            inputs = [own["grad"], own["middle"], *own["n2"], second_gain, *own["att"]]
            inputs += [attend_scale, out_bias, own["q"], own["k"], own["v"], own["probs"]]
            outs = run(
                functools.partial(attend_backward, layer),
                inputs + attend_weights,
                [whole(v) for v in inputs] + [ANYWHERE] * 8,
                [state, act, head, head, head, act, ((4, width), F32), ((2, features), F32)],
                attend_scratch
                + [pltpu.VMEM((tokens, features), BF16), pltpu.SemaphoreType.DMA((8,))],
                "attend_backward",
                2 * attend_flops,
            )
            own.update(zip(("grad_middle", "grad_att", "gq", "gk", "gv"), outs))
            n1 = (outs[5], swap_x(outs[5]))
            carry[m] = (own["grad_middle"], own["current"], *n1)
            attend_sums.append(outs[6:])
        normed = [kept[m]["normed"] for m in samples]
        grad_att = [kept[m]["grad_att"] for m in samples]

        def attend_pairs(offset):
            return [
                (normed, spans("gq", heads_half, offset)),
                (normed, spans("gk", heads_half, offset)),
                (normed, spans("gv", heads_half, offset)),
                (grad_att, spans("mixed", heads_half, offset)),
            ]

        given = weight_grads(attend_pairs(heads_half), places_attend, None, 1, "attend_grads_given")
        taken = [swap_core(value) for value in given]
        part = weight_grads(attend_pairs(0), places_attend, taken, 1, "attend_grads")
        one, two = reduce_pair(
            jnp.concatenate(part[:2], axis=1), jnp.concatenate(part[2:], axis=1)
        )
        q_grad, k_grad = one[:, :heads_half], one[:, heads_half:]
        v_grad, o_grad = two[:, :heads_half], two[:, heads_half:]
        grads[layer] = (q_grad, k_grad, v_grad, o_grad, up_grad, down_grad)
        smalls[layer] = (
            sum(s[0] for s in feed_sums),
            sum(s[1] for s in feed_sums),
            sum(s[0] for s in attend_sums),
            sum(s[1] for s in attend_sums),
        )

    inputs_grad = []
    final_sums = []
    for m in samples:
        inputs = [*carry[m], first_gain]
        outs = run(
            finish_backward,
            inputs,
            [whole(v) for v in inputs],
            [state, ((2, width), F32)],
            [],
            "finish_backward",
            tokens * width,
        )
        inputs_grad.append(outs[0])
        final_sums.append(outs[1])
    final_sums = sum(final_sums)

    common = []
    narrow_own, narrow_other = [], []
    for layer in range(layers):
        feed_rows, feed_wide, attend_rows, attend_wide = smalls[layer]
        first_rows = final_sums if layer == 0 else smalls[layer - 1][0][2:4]
        common += [first_rows, attend_rows, feed_rows[0:2]]
        for target, start in ((narrow_own, 0), (narrow_other, 1)):
            a, b = start * heads_half, start * hidden_half
            target += [
                feed_wide[:, b : b + hidden_half].reshape(-1),
                attend_wide[:, a : a + heads_half].reshape(-1),
            ]
    common = jnp.concatenate(common, axis=0)
    common_count = common.shape[0]
    sent = jnp.concatenate([common.reshape(-1), *narrow_other])
    held = jnp.concatenate([common.reshape(-1), *narrow_own])
    total = held + swap_core(sent)
    split = common_count * width
    pieces = [total[:split].reshape(common_count, n, width // n).transpose(1, 0, 2).reshape(n, -1)]
    at = split
    lengths = []
    for layer in range(layers):
        for length in (hidden_half, heads_half, heads_half):
            pieces.append(total[at : at + length].reshape(n, length // n))
            lengths.append(length // n)
            at += length
    packed = jnp.concatenate(pieces, axis=1)
    if ring:
        mine = small_scatter(packed, n)
    else:
        mine = lax.psum_scatter(packed, "dp", scatter_dimension=0, tiled=True).reshape(-1)
    each = width // n
    vectors = mine[: common_count * each].reshape(layers, 8, each)
    at = common_count * each
    narrow = []
    for length in lengths:
        narrow.append(mine[at : at + length])
        at += length
    up_bias_grad = jnp.stack([narrow[3 * layer] for layer in range(layers)])
    query_bias_grad = jnp.stack([narrow[3 * layer + 1] for layer in range(layers)])
    value_bias_grad = jnp.stack([narrow[3 * layer + 2] for layer in range(layers)])

    def join(values):
        mine_now = jnp.stack([v.reshape(slots, width) for v in values])
        theirs = jnp.stack([swap_core(v).reshape(slots, width) for v in values])
        low = core == 0
        return jnp.concatenate(
            [jnp.where(low, mine_now, theirs), jnp.where(low, theirs, mine_now)], axis=0
        )

    stacked = [jnp.stack([grads[layer][i] for layer in range(layers)]) for i in range(6)]
    return (
        join(results),
        join(inputs_grad),
        vectors[:, 0],
        vectors[:, 1],
        stacked[0],
        stacked[1],
        stacked[2],
        query_bias_grad,
        value_bias_grad,
        stacked[3],
        vectors[:, 2],
        vectors[:, 3],
        vectors[:, 4],
        vectors[:, 5],
        stacked[4],
        up_bias_grad,
        stacked[5],
        vectors[:, 6],
        vectors[:, 7],
    )


def solution(mesh):
    return jax.shard_map(
        functools.partial(per_device, mesh.shape["dp"]),
        mesh=mesh,
        in_specs=(
            P("dp", None, None),
            P("dp", None),
            P(),
            P(),
            P(None, None, "mp"),
            P(None, None, "mp"),
            P(None, None, "mp"),
            P(None, "mp"),
            P(None, "mp"),
            P(None, None, "mp"),
            P(),
            P(),
            P(),
            P(),
            P(None, None, "mp"),
            P(None, "mp"),
            P(None, None, "mp"),
            P(),
            P(),
            P("dp", None, None),
        ),
        out_specs=(
            P("dp", None, None),
            P("dp", None, None),
            P(None, "dp"),
            P(None, "dp"),
            P(None, "dp", "mp"),
            P(None, "dp", "mp"),
            P(None, "dp", "mp"),
            P(None, ("mp", "dp")),
            P(None, ("mp", "dp")),
            P(None, "dp", "mp"),
            P(None, "dp"),
            P(None, "dp"),
            P(None, "dp"),
            P(None, "dp"),
            P(None, "dp", "mp"),
            P(None, ("mp", "dp")),
            P(None, "dp", "mp"),
            P(None, "dp"),
            P(None, "dp"),
        ),
        check_vma=False,
    )
```

```python
import functools
import math

import jax
import jax.numpy as jnp
from jax import lax
from jax.experimental import pallas as pl
from jax.experimental.pallas import tpu as pltpu
from jax.sharding import Mesh
from jax.sharding import PartitionSpec as P

HD = 64
EPSILON = 1e-06
MASKED = -1e30
F32 = jnp.float32
BF16 = jnp.bfloat16
CONTRACT_LAST = (((1,), (1,)), ((), ()))
CONTRACT_ROWS = (((0,), (0,)), ((), ()))
MIB = 1024 * 1024
MICROSECOND = 3_690_000
SAMPLE = 2
SMALL = 32
DP, X, CORE = "dp", "x", "core"
SHARED = (X, CORE)
FAR, OUT, FUNC = "_hbm", "_out", "func"
BLOCK = 256


def dot(a, b):
    return jnp.dot(a, b, preferred_element_type=F32)


def dot_last(a, b):
    return lax.dot_general(a, b, CONTRACT_LAST, preferred_element_type=F32)


def dot_rows(a, b):
    return lax.dot_general(a, b, CONTRACT_ROWS, preferred_element_type=F32)


def normalise(values):
    center = values - jnp.mean(values, axis=-1, keepdims=True)
    spread = jnp.mean(center * center, axis=-1, keepdims=True)
    factor = lax.rsqrt(spread + EPSILON)
    return center * factor, factor


def norm_back(hat, factor, gain, grad):
    inner = grad * gain
    first = jnp.mean(inner, axis=-1, keepdims=True)
    second = jnp.mean(inner * hat, axis=-1, keepdims=True)
    return factor * (inner - first - hat * second)


def column_sum(values):
    return jnp.sum(values, axis=0, keepdims=True)


def both(mine, theirs):
    return mine[...].astype(F32) + theirs[...].astype(F32)


def sides(pair, first, axis):
    zero = jnp.zeros_like(pair)
    return jnp.concatenate([jnp.where(first, pair, zero), jnp.where(first, zero, pair)], axis=axis)


def term(*numbers):
    return "t" + "_".join(map(str, numbers))


class Refs:
    def __init__(self, names, refs):
        self.__dict__.update(zip(names, refs))
        self.names = {id(ref): name for name, ref in zip(names, refs)}
        self.loading, self.saving = {}, []

    def load(self, plan):
        for index, (name, target, part, place) in enumerate(plan):
            source = getattr(self, name)
            room = getattr(self, target)
            copy = pltpu.make_async_copy(
                source if part is None else source.at[part],
                room if place is None else room.at[place],
                self.load_sems.at[index],
            )
            copy.start()
            self.loading.setdefault(target, []).append(copy)

    def numbered(self, kind):
        found = []
        while hasattr(self, term(kind, len(found))):
            found.append(getattr(self, term(kind, len(found))))
        return found

    def need(self, *refs):
        for ref in refs:
            for copy in self.loading.pop(self.names[id(ref)], ()):
                copy.wait()

    def save(self, source, part=None):
        target = self.__dict__.get(self.names[id(source)] + OUT)
        if target is None:
            return
        if part is not None:
            source, target = source.at[part], target.at[part]
        copy = pltpu.make_async_copy(source, target, self.save_sems.at[len(self.saving)])
        copy.start()
        self.saving.append(copy)

    def finish(self):
        for name in list(self.loading):
            self.need(getattr(self, name))
        for copy in self.saving:
            copy.wait()


INSIDE = pl.BlockSpec(memory_space=pltpu.VMEM)
OUTSIDE = pl.BlockSpec(memory_space=pltpu.HBM)
SCALARS = pl.BlockSpec(memory_space=pltpu.SMEM)


class Chain:
    def __init__(self):
        self.mark = None


def title(body):
    while hasattr(body, FUNC):
        body = getattr(body, FUNC)
    return body.__name__


def run(chain, body, cost, near, far, inner, saved, room, table=None, limit=16, whole={}, over=None):
    names, values, in_specs = [], [], []
    if table is not None:
        names.append("table")
        values.append(table)
        in_specs.append(SCALARS)
    for key, value in near.items():
        names.append(key)
        values.append(pltpu.with_memory_space_constraint(value, pltpu.VMEM))
        in_specs.append(INSIDE)
    for key, value in far.items():
        names.append(key)
        values.append(pltpu.with_memory_space_constraint(value, pltpu.HBM))
        in_specs.append(OUTSIDE)
    aliases = {}
    if over is not None:
        aliases = {len(values): len(inner) + len(saved)}
        names.append("over")
        values.append(pltpu.with_memory_space_constraint(over, pltpu.HBM))
        in_specs.append(OUTSIDE)
    if chain.mark is not None:
        names.append("mark_in")
        values.append(chain.mark)
        in_specs.append(pl.BlockSpec(memory_space=pl.ANY))
    out_shape, out_specs = [], []
    for key, (shape, kind) in inner.items():
        names.append(key)
        out_shape.append(pltpu.VMEM(shape, kind))
        out_specs.append(INSIDE)
    for key, (shape, kind) in saved.items():
        names.append(key + OUT)
        out_shape.append(pltpu.HBM(shape, kind))
        out_specs.append(OUTSIDE)
    for key, (shape, kind) in whole.items():
        names.append(key + OUT)
        out_shape.append(pltpu.HBM(shape, kind))
        out_specs.append(OUTSIDE)
    names.append("mark")
    out_shape.append(jax.ShapeDtypeStruct((8, 128), F32))
    out_specs.append(pl.BlockSpec(memory_space=pl.ANY))
    scratch = []
    for key, (shape, kind) in {**saved, **room}.items():
        names.append(key)
        scratch.append(pltpu.VMEM(shape, kind))
    names += ["load_sems", "save_sems"]
    scratch += [pltpu.SemaphoreType.DMA((32,)), pltpu.SemaphoreType.DMA((32,))]

    def kernel(*refs):
        body(Refs(names, refs))

    outs = pl.pallas_call(
        kernel,
        out_shape=out_shape,
        in_specs=in_specs,
        out_specs=out_specs,
        scratch_shapes=scratch,
        input_output_aliases=aliases,
        compiler_params=pltpu.CompilerParams(vmem_limit_bytes=limit * MIB),
        cost_estimate=pl.CostEstimate(flops=1, bytes_accessed=cost * MICROSECOND, transcendentals=0),
        name=title(body),
    )(*values)
    chain.mark = outs[-1]
    return dict(zip([*inner, *saved, *whole], outs))


def stage(layer, names, r):
    plan = []
    for owner, target in (("_own", "w"), ("_other", "x")):
        at = 0
        for name in names:
            width = getattr(r, name + owner).shape[2]
            plan.append((name + owner, target, layer, (slice(None), slice(at, at + width))))
            at += width
    r.load(plan)
    r.finish()


def piece(r, side, index):
    return (r.w, r.x)[side][:, index * BLOCK : (index + 1) * BLOCK]


def attend_forward(layer, r):
    now = slice(layer, layer + 1)
    half = r.query.shape[1] // 2
    if layer == 0:
        values = r.source[...].astype(F32)
    else:
        last = slice(layer - 1, layer)
        fed = both(r.mine, r.theirs)
        values = r.middle[...] + r.feed_scale[last] * (fed + r.down_bias[last])
        r.fed[...] = fed.astype(BF16)
        r.save(r.fed)
    r.current[...] = values
    hat, factor = normalise(values)
    r.factor[...] = jnp.broadcast_to(factor, r.factor.shape)
    r.save(r.factor)
    normed = (hat * r.gain[now] + r.shift[now]).astype(BF16)
    r.normed[...] = normed
    r.save(r.normed)
    tokens = values.shape[0]
    for index, (target, bias) in enumerate(
        ((r.query, r.query_bias), (r.key, None), (r.value, r.value_bias))
    ):
        for side in range(2):
            cols = slice(side * half, (side + 1) * half)
            found = dot(normed, piece(r, side, index))
            if bias is not None:
                found = found + bias[now, cols]
            target[:, cols] = found.astype(BF16)
    r.save(r.query)
    r.save(r.key)
    r.save(r.value)
    lane = lax.broadcasted_iota(jnp.int32, (tokens, 2 * HD), 1)
    first = lane < HD
    scale = jnp.asarray(HD ** (-0.5), BF16)
    blocked = jnp.concatenate([r.mask[...], r.mask[...]], axis=0)
    for pair in range(half // HD):
        cols = slice(pair * 2 * HD, (pair + 1) * 2 * HD)
        scores = dot_last(sides(r.query[:, cols] * scale, first, 0), r.key[:, cols]) + blocked
        top = jnp.max(scores, axis=-1, keepdims=True)
        weights = jnp.exp(scores - top)
        total = jnp.sum(weights, axis=-1, keepdims=True)
        probs = (weights * (1.0 / total)).astype(BF16)
        r.probs[2 * pair] = probs[:tokens]
        r.probs[2 * pair + 1] = probs[tokens:]
        r.save(r.probs, slice(2 * pair, 2 * pair + 2))
        flat = jnp.concatenate([probs[:tokens], probs[tokens:]], axis=1)
        r.mixed[:, cols] = dot(flat, sides(r.value[:, cols], first, 0)).astype(BF16)
    r.save(r.mixed)
    contract(r, r.mixed, slice(3 * half, 4 * half), r.part)
    r.finish()


def contract(r, left, lanes, target):
    for start in range(0, target.shape[1], BLOCK):
        rows = slice(start, start + BLOCK)
        right = jnp.concatenate([r.w[rows, lanes], r.x[rows, lanes]], axis=1)
        target[:, rows] = dot_last(left[...], right).astype(BF16)


def block_of(r, index, start):
    half = r.w.shape[1] // 2
    return piece(r, start // half, (index * half + start % half) // BLOCK)


def half_of(r, index):
    half = r.w.shape[1] // 2
    return slice(index * half, (index + 1) * half)


def feed_enter(layer, r):
    now = slice(layer, layer + 1)
    attended = both(r.mine, r.theirs)
    values = r.current[...] + r.attend_scale[now] * (attended + r.out_bias[now])
    r.middle[...] = values
    r.save(r.middle)
    r.att[...] = attended.astype(BF16)
    r.save(r.att)
    hat, factor = normalise(values)
    r.factor2[...] = jnp.broadcast_to(factor, r.factor2.shape)
    r.save(r.factor2)
    normed = (hat * r.gain[now] + r.shift[now]).astype(BF16)
    r.normed2[...] = normed
    r.save(r.normed2)
    return normed


def expand(layer, r, normed, cols):
    before = dot(normed, block_of(r, 0, cols.start)) + r.up_bias[layer : layer + 1, cols]
    lower = 0.5 + 0.5 * lax.erf(before * math.sqrt(0.5))
    bell = jnp.exp(-0.5 * before * before) * (1.0 / math.sqrt(2.0 * math.pi))
    return (before * lower).astype(BF16), lower + before * bell


def feed_forward(layer, r):
    normed = feed_enter(layer, r)
    for start in range(0, r.act.shape[1], BLOCK):
        cols = slice(start, start + BLOCK)
        active, slope = expand(layer, r, normed, cols)
        r.act[:, cols] = active
        r.save(r.act, (slice(None), cols))
        r.slope[:, cols] = slope.astype(BF16)
        r.save(r.slope, (slice(None), cols))
    contract(r, r.act, half_of(r, 1), r.part)
    r.finish()


def feed_both(layer, r):
    now = slice(layer, layer + 1)
    scaled = r.feed_scale[now] * r.grad[...].astype(F32)
    grad_fed = scaled.astype(BF16)
    r.grad_fed[...] = grad_fed
    r.save(r.grad_fed)
    r.sums[...] = column_sum(scaled)
    normed = feed_enter(layer, r)
    for start in range(0, r.act.shape[1], BLOCK):
        cols = slice(start, start + BLOCK)
        active, slope = expand(layer, r, normed, cols)
        r.act[:, cols] = active
        r.save(r.act, (slice(None), cols))
        before = (dot(grad_fed, block_of(r, 1, start)) * slope).astype(BF16)
        r.before[:, cols] = before
        r.save(r.before, (slice(None), cols))
        r.wide_sums[:, cols] = column_sum(before.astype(F32))
    contract(r, r.act, half_of(r, 1), r.fed_part)
    r.save(r.fed_part)
    contract(r, r.before, half_of(r, 0), r.part)
    r.finish()


def finish_forward(layer, r):
    now = slice(layer, layer + 1)
    r.need(r.mine, r.theirs)
    fed = both(r.mine, r.theirs) + r.down_bias[now]
    r.need(r.middle)
    r.result[...] = (r.middle[...] + r.feed_scale[now] * fed).astype(BF16)
    r.save(r.result)
    r.sums[...] = column_sum(r.grad[...].astype(F32) * fed)
    r.finish()


def norm_enter(r, normed, factor, gain, shift):
    grad_normed = both(r.mine, r.theirs)
    hat = (normed[...].astype(F32) - shift) * (1.0 / gain)
    grad = norm_back(hat, factor[:, 0:1], gain, grad_normed)
    return grad, column_sum(grad_normed * hat), column_sum(grad_normed)


def feed_backward(layer, r):
    now = slice(layer, layer + 1)
    deep = slice(layer + 1, layer + 2)
    r.need(r.normed, r.factor)
    step, gain_sum, shift_sum = norm_enter(r, r.normed, r.factor, r.gain[deep], r.shift[deep])
    r.need(r.after)
    grad = r.after[...] + step
    r.grad[...] = grad
    r.save(r.grad)
    scaled = r.feed_scale[now] * grad
    grad_fed = scaled.astype(BF16)
    r.grad_fed[...] = grad_fed
    r.save(r.grad_fed)
    r.need(r.fed, r.slope)
    r.sums[0:1] = column_sum(scaled)
    r.sums[1:2] = column_sum(grad * (r.fed[...].astype(F32) + r.down_bias[now]))
    r.sums[2:3] = gain_sum
    r.sums[3:4] = shift_sum
    for start in range(0, r.before.shape[1], BLOCK):
        cols = slice(start, start + BLOCK)
        grad_active = dot(grad_fed, block_of(r, 1, start))
        before = (grad_active * r.slope[:, cols].astype(F32)).astype(BF16)
        r.before[:, cols] = before
        r.save(r.before, (slice(None), cols))
        r.wide_sums[:, cols] = column_sum(before.astype(F32))
    contract(r, r.before, half_of(r, 0), r.part)
    r.finish()


def attend_backward(layer, r):
    now = slice(layer, layer + 1)
    half = r.gq.shape[1] // 2
    r.need(r.normed2, r.factor2)
    step, gain_sum, shift_sum = norm_enter(r, r.normed2, r.factor2, r.gain[now], r.shift[now])
    r.need(r.grad)
    grad = r.grad[...].astype(F32) + step
    r.grad_middle[...] = grad
    r.save(r.grad_middle)
    scaled = r.attend_scale[now] * grad
    grad_att = scaled.astype(BF16)
    r.grad_att[...] = grad_att
    r.save(r.grad_att)
    r.need(r.att)
    r.sums[0:1] = column_sum(scaled)
    r.sums[1:2] = column_sum(grad * (r.att[...].astype(F32) + r.out_bias[now]))
    r.sums[2:3] = gain_sum
    r.sums[3:4] = shift_sum
    for side in range(2):
        cols = slice(side * half, (side + 1) * half)
        r.grad_mixed[:, cols] = dot(grad_att, piece(r, side, 3)).astype(BF16)
    r.need(r.value, r.probs, r.key, r.query)
    tokens = grad.shape[0]
    lane = lax.broadcasted_iota(jnp.int32, (tokens, 2 * HD), 1)
    first = lane < HD
    scale = HD ** (-0.5)
    for pair in range(half // HD):
        cols = slice(pair * 2 * HD, (pair + 1) * 2 * HD)
        mixed = sides(r.grad_mixed[:, cols], first, 0)
        probs_low = jnp.concatenate([r.probs[2 * pair], r.probs[2 * pair + 1]], axis=0)
        grad_probs = dot_last(mixed, r.value[:, cols])
        probs = probs_low.astype(F32)
        weighted = probs * grad_probs
        row = jnp.sum(weighted, axis=-1, keepdims=True)
        grad_scores = (weighted - probs * row).astype(BF16)
        flat = jnp.concatenate([grad_scores[:tokens], grad_scores[tokens:]], axis=1)
        r.gq[:, cols] = (dot(flat, sides(r.key[:, cols], first, 0)) * scale).astype(BF16)
        r.gk[:, cols] = (dot_rows(grad_scores, sides(r.query[:, cols], first, 0)) * scale).astype(
            BF16
        )
        r.gv[:, cols] = dot_rows(probs_low, mixed).astype(BF16)
    r.save(r.gq)
    r.save(r.gk)
    r.save(r.gv)
    r.wide_sums[0:1] = column_sum(r.gq[...].astype(F32))
    r.wide_sums[1:2] = column_sum(r.gv[...].astype(F32))
    left = [
        grad_now[:, side * half : (side + 1) * half]
        for side in range(2)
        for grad_now in (r.gq, r.gk, r.gv)
    ]
    left = jnp.concatenate(left, axis=1)
    for start in range(0, r.part.shape[1], BLOCK):
        cols = slice(start, start + BLOCK)
        right = jnp.concatenate([r.w[cols, : 3 * half], r.x[cols, : 3 * half]], axis=1)
        r.part[:, cols] = dot_last(left, right).astype(BF16)
    r.finish()


def finish_backward(r):
    r.need(r.normed, r.factor)
    step, gain_sum, shift_sum = norm_enter(r, r.normed, r.factor, r.gain[0:1], r.shift[0:1])
    r.need(r.after)
    r.input_grad[...] = r.after[...] + step
    r.save(r.input_grad)
    r.sums[0:1] = gain_sum
    r.sums[1:2] = shift_sum
    r.finish()


def with_loads(body, plan):
    def loaded(r):
        r.load(plan)
        body(r)

    loaded.func = body
    return loaded


def simple_plan(names):
    return [(name + FAR, name, None, None) for name in names]


def weight_grad(chunks, groups, column, r):
    rows = getattr(r, groups[0][0] + str(0)).shape[1] // chunks
    split = chunks // 2
    r.gives = r.numbered(0)
    copies = []
    for side in (1, 0):
        for step in range(0, chunks, 2):
            at = 0
            if column is not None:
                places = [(step + way) * rows for way in range(2)]
                target, base = r.block, (side * chunks + step) * rows
            else:
                places = [pl.multiple_of(r.table[step + way] * rows, rows) for way in range(2)]
                if side == 0:
                    target, base = (r.own_send, r.own_keep)[step // split], step % split * rows
                else:
                    parts = len(r.gives)
                    index, base = divmod(step * rows, chunks * rows // parts)
                    target = r.gives[index]
            where = slice(base, base + 2 * rows)
            for left_name, rights in groups:
                r.need(*(getattr(r, left_name + str(m)) for m in range(SAMPLE)))
                left = jnp.concatenate(
                    [
                        jnp.concatenate(
                            [
                                getattr(r, left_name + str(m))[:, pl.ds(place, rows)]
                                for place in places
                            ],
                            axis=1,
                        )
                        for m in range(SAMPLE)
                    ],
                    axis=0,
                )
                for right_name in rights:
                    r.need(*(getattr(r, right_name + str(m)) for m in range(SAMPLE)))
                    half = getattr(r, right_name + str(0)).shape[1] // 2
                    for offset in range(0, half, BLOCK):
                        lanes = slice(side * half + offset, side * half + offset + BLOCK)
                        right = jnp.concatenate(
                            [getattr(r, right_name + str(m))[:, lanes] for m in range(SAMPLE)],
                            axis=0,
                        )
                        target[where, at + offset : at + offset + BLOCK] = dot_rows(
                            left, right
                        ).astype(BF16)
                    at += half
            if column is None:
                r.save(target, where)
                continue
            owner = r.table[0] if side == 0 else 1 - r.table[0]
            first = pl.multiple_of((owner * chunks + step) * rows, 2 * rows)
            copy = pltpu.make_async_copy(
                target.at[where],
                r.bulk_out.at[pl.ds(first, 2 * rows), column : column + at],
                r.save_sems.at[len(copies)],
            )
            copy.start()
            copies.append(copy)
    for copy in copies:
        copy.wait()
    r.finish()


def add_send(r):
    at = 0
    for got in r.numbered(0):
        rows = slice(at, min(at + got.shape[0], r.total.shape[0]))
        at = rows.stop
        r.total[rows] = both(r.own_send.at[rows], got.at[: rows.stop - rows.start]).astype(BF16)


def add_first(r):
    gots = r.numbered(0)
    r.need(r.own_keep, *gots)
    rows = r.leave.shape[0]
    for side, target in enumerate((r.leave, r.stay)):
        where = slice(side * rows, (side + 1) * rows)
        part = where if len(gots) == 1 else slice(0, rows)
        total = both(r.own_keep.at[where], gots[side % len(gots)].at[part])
        target[...] = (total + r.arrived[where].astype(F32)).astype(BF16)
    r.finish()


def add_second(r):
    rows = r.leave.shape[0]
    for target, where in ((r.leave, slice(0, rows)), (r.stay, slice(rows, 2 * rows))):
        target[...] = both(r.keep.at[where], r.arrived.at[where]).astype(BF16)


def add_third(r):
    r.found[...] = both(r.keep, r.arrived)
    r.save(r.found)
    r.finish()


def add_last(layers, pieces, names, r):
    each = len(names) // pieces
    width = getattr(r, names[0]).shape[2]
    for layer in reversed(range(layers)):
        for piece in range(pieces):
            if layer > 0:
                found = getattr(r, term(layer, piece, 0))
                r.need(found)
                total = found[...].astype(F32)
            else:
                total = both(*(getattr(r, term(layer, piece, index)) for index in range(2)))
            for index, name in enumerate(names[piece * each : (piece + 1) * each]):
                getattr(r, name)[layer] = total[:, index * width : (index + 1) * width]
                r.save(getattr(r, name), layer)
    r.finish()


def place_rows(r):
    core = r.table[0]
    copies = []
    for index in range(SAMPLE):
        for side, owner in enumerate((core, 1 - core)):
            copy = pltpu.make_async_copy(
                getattr(r, term(side, index)),
                r.whole_out.at[owner * SAMPLE + index],
                r.save_sems.at[len(copies)],
            )
            copy.start()
            copies.append(copy)
    for copy in copies:
        copy.wait()


def gather_small(layers, heads_half, hidden_half, r):
    slots, _, each = r.own.shape

    def total(*numbers):
        return sum(getattr(r, term(*numbers, m))[...] for m in range(SAMPLE))

    common, up, wide = [], [[], []], [[], []]
    for layer in range(layers):
        feed, attend = total(layer, 2), total(layer, 0)
        if layer == 0:
            first = total(layers, 0)
        else:
            first = total(layer - 1, 2)[2:4]
        if layer == layers - 1:
            feed = jnp.concatenate([feed, total(layers, 1)], axis=0)
        common += [first, attend, feed[0:2]]
        feed_wide, attend_wide = total(layer, 3), total(layer, 1)
        for side in range(2):
            up[side].append(feed_wide[:, side * hidden_half : (side + 1) * hidden_half])
            wide[side].append(attend_wide[:, side * heads_half : (side + 1) * heads_half])
    common = jnp.concatenate(common, axis=0)
    r.common[...] = common
    for side in range(2):
        r.up[...] = jnp.concatenate(up[side], axis=0)
        target = (r.own, r.give)[side]
        rows = jnp.concatenate(wide[side], axis=0)
        for slot in range(slots):
            place = pl.ds(pl.multiple_of(r.table[slot] * each, each), each)
            target[slot] = jnp.zeros_like(target[slot])
            target[slot, : 8 * layers] = r.common[:, place]
            target[slot, 8 * layers : 9 * layers] = r.up[:, place]
            for index in range(2 * layers):
                for part in range(heads_half // each):
                    at = 9 * layers + index * (heads_half // each) + part
                    target[slot, at : at + 1] = rows[
                        index : index + 1, part * each : (part + 1) * each
                    ]


def per_device(
    n,
    activations,
    segments,
    first_gain,
    first_shift,
    query_weight,
    key_weight,
    value_weight,
    query_bias,
    value_bias,
    out_weight,
    out_bias,
    attend_scale,
    second_gain,
    second_shift,
    up_weight,
    up_bias,
    down_weight,
    down_bias,
    feed_scale,
    cotangent,
):
    rows, slots, width = activations.shape
    layers = first_gain.shape[0]
    core = lax.axis_index(CORE)
    mine_rows = rows // 2
    tokens = slots
    assert mine_rows == SAMPLE
    heads_half = query_weight.shape[2]
    hidden_half = up_weight.shape[2]
    features = 2 * heads_half
    hidden = 2 * hidden_half
    heads = features // HD
    samples = range(SAMPLE)
    direct = n == 8

    def swap_core(value):
        return lax.ppermute(value, CORE, [(0, 1), (1, 0)])

    def swap_x(value):
        return lax.ppermute(value, X, [(0, 1), (1, 0)])

    biases = jnp.concatenate([query_bias, value_bias, up_bias], axis=1)
    own = dict(wq=query_weight, wk=key_weight, wv=value_weight, wo=out_weight)
    own.update(wu=up_weight, wd=down_weight)
    biases_other = swap_core(biases)
    chain = Chain()

    attend_names = ("wq", "wk", "wv", "wo")
    feed_names = ("wu", "wd")
    other = {name: swap_core(own[name]) for name in attend_names}
    held_back = [own[name] for name in feed_names]
    held_back, other, biases_other = lax.optimization_barrier((held_back, other, biases_other))
    other.update({name: swap_core(value) for name, value in zip(feed_names, held_back)})

    def staged(layer, names):
        far = {}
        for name in names:
            far[name + "_own"], far[name + "_other"] = own[name], other[name]
        total = sum(own[name].shape[2] for name in names)
        return run(
            chain,
            functools.partial(stage, layer, names),
            total // 400,
            {},
            far,
            {side: ((width, total), BF16) for side in "wx"},
            {},
            {},
            limit=2,
        )

    pieces = jnp.concatenate([biases, biases_other], axis=1)
    span = heads_half * 2 + hidden_half
    query_bias_all = jnp.concatenate([pieces[:, :heads_half], pieces[:, span : span + heads_half]], 1)
    value_bias_all = jnp.concatenate(
        [pieces[:, heads_half:features], pieces[:, span + heads_half : span + features]], 1
    )
    up_bias_all = jnp.concatenate([pieces[:, features:span], pieces[:, span + features :]], 1)

    def own_rows(value):
        start = (core * mine_rows,) + (0,) * (value.ndim - 1)
        return lax.dynamic_slice(value, start, (mine_rows,) + value.shape[1:])

    own_segments = own_rows(segments)
    same = own_segments[:, :, None] == own_segments[:, None, :]
    held = ("grad", "query", "key", "value", "probs", "normed2", "att", "factor2")
    held += ("act", "before", "grad_fed")
    masks = jnp.where(same, 0.0, MASKED).astype(F32)
    own_input = own_rows(activations)
    own_cotangent = own_rows(cotangent)

    act = ((tokens, width), BF16)
    state = ((tokens, width), F32)
    head = ((tokens, features), BF16)
    hid = ((tokens, hidden), BF16)
    column = ((tokens, 128), F32)
    probs_shape = ((heads, slots, slots), BF16)

    kept = [[None] * SAMPLE for _ in range(layers)]
    feed_sums = [[None] * SAMPLE for _ in range(layers)]
    for layer in range(layers):
        last = layer == layers - 1
        attend_weights = staged(layer, attend_names)
        for m in samples:
            near = dict(mask=masks[m], gain=first_gain, shift=first_shift)
            near.update(query_bias=query_bias_all, value_bias=value_bias_all)
            near.update(attend_weights)
            saved = dict(
                normed=act, query=head, key=head, value=head, probs=probs_shape, mixed=head
            )
            saved["factor"] = column
            if layer == 0:
                near["source"] = own_input[m]
            else:
                before = kept[layer - 1][m]
                near.update(middle=before["middle"], mine=before["fed_mine"])
                near.update(theirs=before["fed_theirs"], feed_scale=feed_scale, down_bias=down_bias)
                saved["fed"] = act
            inner = dict(current=state, part=act)
            if last:
                inner.update({name: saved.pop(name) for name in list(saved) if name in held})
            outs = run(
                chain,
                functools.partial(attend_forward, layer),
                6,
                near,
                {},
                inner,
                saved,
                {},
            )
            if layer > 0:
                before["fed"] = outs.pop("fed")
            kept[layer][m] = now = dict(outs)
            now["mine"], now["theirs"] = outs["part"], swap_x(outs["part"])
        feed_weights = staged(layer, feed_names)
        for m in samples:
            now = kept[layer][m]
            near = {name: now[name] for name in ("current", "mine", "theirs")}
            near.update(attend_scale=attend_scale, out_bias=out_bias, up_bias=up_bias_all)
            near.update(gain=second_gain, shift=second_shift)
            near.update(feed_weights)
            inner = dict(middle=state, part=act)
            saved = dict(normed2=act, att=act, factor2=column, act=hid)
            if not last:
                saved["slope"] = hid
                body = feed_forward
            else:
                near.update(grad=own_cotangent[m], feed_scale=feed_scale)
                del inner["middle"]
                inner.update(sums=((1, width), F32), wide_sums=((1, hidden), F32))
                saved.update(middle=state, fed_part=act, grad_fed=act, before=hid)
                inner.update({name: saved.pop(name) for name in list(saved) if name in held})
                body = feed_both
            outs = run(
                chain,
                functools.partial(body, layer),
                11 if last else 7,
                near,
                {},
                inner,
                saved,
                {},
            )
            now.update(outs)
            if not last:
                now["fed_mine"], now["fed_theirs"] = outs["part"], swap_x(outs["part"])
            else:
                now["mine"], now["theirs"] = outs["part"], swap_x(outs["part"])
                now["fed_mine"] = outs["fed_part"]
                now["grad"] = own_cotangent[m]
                feed_sums[layer][m] = (outs["sums"], outs["wide_sums"])

    me = lax.axis_index(DP)
    def order_of(bits):
        if not direct:
            return jnp.arange(8).astype(jnp.int32)
        a, b, c = bits
        keep = (b + c, b, c, 0)
        return (me ^ jnp.array([a + r for r in keep] + list(keep))).astype(jnp.int32)

    table = order_of((1, 2, 4))
    len_table = 8

    core_now = core.astype(jnp.int32).reshape(1)
    half_shape = ((width // 2, 4 * heads_half), BF16)
    assert hidden_half == 4 * heads_half

    def products(layer, groups, column=None, bulk=None, bits=(1, 2, 4), parts=1):
        near, far, room, plan = {}, {}, {}, []
        for left, rights in groups:
            for name in [left, *rights]:
                for m in samples:
                    value = kept[layer][m][name]
                    if name in held and layer == layers - 1:
                        near[name + str(m)] = value
                    else:
                        far[name + FAR + str(m)] = value
                        room[name + str(m)] = (value.shape, BF16)
                        plan.append((name + FAR + str(m), name + str(m), None, None))
        if column is not None:
            return run(
                chain,
                with_loads(functools.partial(weight_grad, 8, groups, column), plan),
                6,
                near,
                far,
                {},
                {},
                dict(room, block=((2 * width, 4 * heads_half), BF16)),
                table=core_now,
                whole=dict(bulk=((2 * width, 3 * hidden_half), BF16)),
                over=bulk,
            )["bulk"]
        outs = run(
            chain,
            with_loads(functools.partial(weight_grad, 8, groups, None), plan),
            6,
            near,
            far,
            dict(own_send=half_shape),
            dict(
                {term(0, i): ((width // parts, 4 * heads_half), BF16) for i in range(parts)},
                own_keep=half_shape,
            ),
            room,
            table=order_of(bits),
            limit=16,
        )
        outs["got"] = [swap_core(outs[term(0, i)]) for i in range(parts)]
        outs["bits"] = bits
        return outs

    quarter_shape = ((width // 4, 4 * heads_half), BF16)
    eighth_shape = ((width // 8, 4 * heads_half), BF16)

    def swap_dp(value, bit):
        return lax.ppermute(value, DP, [(i, i ^ bit) for i in range(n)])

    def depart(outs):
        total = run(
            chain,
            add_send,
            1,
            dict(
                {term(0, i): v for i, v in enumerate(outs["got"][: max(1, len(outs["got"]) // 2)])},
                own_send=outs["own_send"],
            ),
            {},
            dict(total=half_shape),
            {},
            {},
            limit=4,
        )["total"]
        if direct:
            outs["arrived"] = swap_dp(total, outs["bits"][0])
        else:
            outs["arrived"] = total

    def second(outs):
        if not direct:
            return
        gots = outs["got"]
        late = gots[len(gots) // 2 :]
        far, loads, plan = dict(own_keep=outs["own_keep"]), dict(own_keep=half_shape), []
        for index, value in enumerate(late):
            far[term(0, index)] = value
            loads[term(0, index)] = ((width // 2 // len(late), 4 * heads_half), BF16)
        for name in far:
            part = slice(width // 2, width) if far[name].shape[0] == width else None
            plan.append((name + FAR, name, part, None))
        found = run(
            chain,
            with_loads(add_first, plan),
            2,
            dict(arrived=outs["arrived"]),
            {name + FAR: value for name, value in far.items()},
            dict(leave=quarter_shape, stay=quarter_shape),
            {},
            loads,
            limit=8,
        )
        outs["keep"], outs["arrived"] = found["stay"], swap_dp(found["leave"], outs["bits"][1])

    def third(outs):
        if not direct:
            return
        found = run(
            chain,
            add_second,
            1,
            dict(arrived=outs["arrived"], keep=outs["keep"]),
            {},
            dict(leave=eighth_shape, stay=eighth_shape),
            {},
            {},
            limit=4,
        )
        outs["keep"], outs["arrived"] = found["stay"], swap_dp(found["leave"], outs["bits"][2])

    def fourth(outs):
        if not direct:
            got = jnp.concatenate(outs["got"], axis=0)
            keep = outs["own_keep"].astype(F32) + got[width // 2 :].astype(F32)
            rows_now = jnp.concatenate([outs["arrived"].astype(F32), keep], axis=0)
            return lax.psum_scatter(rows_now, DP, scatter_dimension=0, tiled=True)
        return run(
            chain,
            add_third,
            1,
            dict(arrived=outs["arrived"], keep=outs["keep"]),
            {},
            {},
            dict(found=(eighth_shape[0], F32)),
            {},
            limit=4,
        )["found"]

    def assemble(found, names, each):
        if not direct:
            found[0] = [fourth(value) for value in found[0]]
            found[1] = [array[:, at : at + hidden_half].astype(F32) for array, at in found[1]]
            joined = jnp.stack([jnp.concatenate(pieces_now, axis=1) for pieces_now in found])
            return [joined[:, :, i * each : (i + 1) * each] for i in range(len(names))]
        near, far, loads, plan = {}, {}, {}, []
        for layer, pieces_now in enumerate(found):
            for piece_now, value in enumerate(pieces_now):
                if layer == 0:
                    near[term(layer, piece_now, 0)] = value["keep"]
                    near[term(layer, piece_now, 1)] = value["arrived"]
                    continue
                name = term(layer, piece_now, 0)
                array, column = value
                far[name + FAR] = array
                shape = (array.shape[0], hidden_half)
                loads[name] = (shape, BF16)
                part = (slice(None), slice(column, column + hidden_half))
                plan.append((name + FAR, name, part, None))
        outs = run(
            chain,
            with_loads(functools.partial(add_last, layers, len(found[0]), names), plan),
            3,
            near,
            far,
            {},
            {name: ((layers, eighth_shape[0][0], each), F32) for name in names},
            loads,
            limit=12,
        )
        return [outs[name] for name in names]

    up_group = [("normed2", ["before"])]
    down_group = [("grad_fed", ["act"])]
    attend_group = [("normed", ["gq", "gk", "gv"]), ("grad_att", ["mixed"])]
    attend_sums = [[None] * SAMPLE for _ in range(layers)]

    def back_feed(layer, m, weights):
        now, deep = kept[layer][m], kept[layer + 1][m]
        near = dict(mine=deep["mine"], theirs=deep["theirs"])
        near.update(gain=first_gain, shift=first_shift)
        near.update(feed_scale=feed_scale, down_bias=down_bias)
        near.update(weights)
        far = dict(normed_hbm=deep["normed"], factor_hbm=deep["factor"])
        far.update(after_hbm=deep["grad_middle"], fed_hbm=now["fed"], slope_hbm=now["slope"])
        loads = dict(normed=act, factor=column, after=state, fed=act, slope=hid)
        outs = run(
            chain,
            with_loads(
                functools.partial(feed_backward, layer),
                simple_plan(loads),
            ),
            8,
            near,
            far,
            dict(part=act, sums=((4, width), F32), wide_sums=((1, hidden), F32)),
            dict(grad=state, grad_fed=act, before=hid),
            loads,
        )
        now.update(outs)
        now["mine"], now["theirs"] = outs["part"], swap_x(outs["part"])
        feed_sums[layer][m] = (outs["sums"], outs["wide_sums"])

    def back_attend(layer, m, weights):
        now = kept[layer][m]
        near = dict(mine=now["mine"], theirs=now["theirs"])
        near.update(gain=second_gain, shift=second_shift)
        near.update(attend_scale=attend_scale, out_bias=out_bias)
        near.update(weights)
        far, loads = {}, {}
        sources = dict(normed2=act, factor2=column, grad=act if layer == layers - 1 else state)
        sources["att"] = act
        sources.update(value=head, probs=probs_shape, key=head, query=head)
        for name, shape in sources.items():
            if layer == layers - 1 and name in held:
                near[name] = now[name]
            else:
                far[name + FAR] = now[name]
                loads[name] = shape
        outs = run(
            chain,
            with_loads(
                functools.partial(attend_backward, layer),
                simple_plan(loads),
            ),
            7,
            near,
            far,
            dict(
                part=act,
                sums=((4, width), F32),
                wide_sums=((2, features), F32),
            ),
            dict(grad_middle=state, grad_att=act, gq=head, gk=head, gv=head),
            dict(loads, grad_mixed=head),
        )
        now.update(outs)
        now["mine"], now["theirs"] = outs["part"], swap_x(outs["part"])
        attend_sums[layer][m] = (outs["sums"], outs["wide_sums"])

    results, last_sums = [], []

    def finish_row(m):
        now = kept[layers - 1][m]
        mine, _ = lax.optimization_barrier((now["fed_mine"], kept[0][SAMPLE - 1]["grad_att"]))
        far = dict(mine_hbm=mine, theirs_hbm=swap_x(mine), middle_hbm=now["middle"])
        near = dict(grad=own_cotangent[m], feed_scale=feed_scale, down_bias=down_bias)
        outs = run(
            chain,
            with_loads(
                functools.partial(finish_forward, layers - 1),
                simple_plan(("mine", "theirs", "middle")),
            ),
            2,
            near,
            far,
            dict(result=act, sums=((1, width), F32)),
            {},
            dict(mine=act, theirs=act, middle=state),
        )
        results.append(outs["result"])
        last_sums.append(outs["sums"])


    inputs_grad, final_sums = [], []

    def final_row(m):
        now = kept[0][m]
        near = dict(mine=now["mine"], theirs=now["theirs"])
        near.update(gain=first_gain, shift=first_shift)
        loads = dict(normed=act, factor=column, after=state)
        now["after"] = now["grad_middle"]
        outs = run(
            chain,
            with_loads(
                finish_backward, simple_plan(loads)
            ),
            2,
            near,
            {name + FAR: now[name] for name in loads},
            dict(input_grad=state, sums=((2, width), F32)),
            {},
            loads,
        )
        inputs_grad.append(outs["input_grad"])
        final_sums.append(outs["sums"])

    def vector_grads():
        near = {}
        for layer in range(layers):
            for m in samples:
                attend_rows, attend_wide = attend_sums[layer][m]
                feed_rows, feed_wide = feed_sums[layer][m]
                for index, value in enumerate((attend_rows, attend_wide, feed_rows, feed_wide)):
                    near[term(layer, index, m)] = value
        for m in samples:
            near[term(layers, 0, m)] = final_sums[m]
            near[term(layers, 1, m)] = last_sums[m]
        each = width // len_table
        small_shape = ((len_table, SMALL, each), F32)
        outs = run(
            chain,
            functools.partial(gather_small, layers, heads_half, hidden_half),
            1,
            near,
            {},
            dict(own=small_shape, give=small_shape),
            {},
            dict(common=((8 * layers, width), F32), up=((layers, hidden_half), F32)),
            table=table,
            limit=4,
        )
        small = outs["own"] + swap_core(outs["give"])
        if direct:
            for bit in (1, 2, 4):
                half = small.shape[0] // 2
                small = small[half:] + swap_dp(small[:half], bit)
            total = small[0]
            vectors = total[: 8 * layers].reshape(layers, 8, each)
            up_bias_grad = total[8 * layers : 9 * layers]
            wide = total[9 * layers :].reshape(-1)[: 4 * layers * each * 2]
        else:
            total = lax.psum(small, DP).transpose(1, 0, 2).reshape(SMALL, -1)
            mine = lax.dynamic_slice_in_dim(total, me * (width // n), width // n, 1)
            vectors = mine[: 8 * layers].reshape(layers, 8, width // n)
            up_bias_grad = mine[8 * layers : 9 * layers]
            wide = total[9 * layers :, :each].reshape(-1)[: 4 * layers * each * 2]
        wide = wide[: 2 * layers * heads_half].reshape(layers, 2, heads_half)
        wide = lax.dynamic_slice_in_dim(wide, me * (heads_half // n), heads_half // n, 2)
        query_bias_grad, value_bias_grad = wide[:, 0], wide[:, 1]
        return vectors, up_bias_grad, query_bias_grad, value_bias_grad

    def join(values):
        near = {term(0, m): values[m] for m in samples}
        near.update({term(1, m): swap_core(values[m]) for m in samples})
        return run(
            chain,
            place_rows,
            3,
            near,
            {},
            {},
            {},
            {},
            table=core_now,
            limit=2,
            whole=dict(whole=((rows, slots, width), values[0].dtype)),
        )["whole"]

    assert layers == 2
    weights = staged(1, attend_names)
    bulk = products(1, up_group, 0)
    back_attend(1, 0, weights)
    bulk = products(1, down_group, hidden_half, bulk)
    back_attend(1, 1, weights)
    weights = staged(0, feed_names)
    back_feed(0, 0, weights)
    bulk = products(1, attend_group, 2 * hidden_half, bulk)
    bulk = lax.psum_scatter(bulk, (CORE, DP), scatter_dimension=0, tiled=True)
    attend_weights = staged(0, attend_names)
    back_feed(0, 1, weights)
    back_attend(0, 0, attend_weights)
    up0 = products(0, up_group, parts=4)
    down0 = products(0, down_group, bits=(2, 1, 4))
    back_attend(0, 1, attend_weights)
    attend0 = products(0, attend_group)
    depart(attend0)
    depart(down0)
    depart(up0)
    finish_row(0)
    second(up0)
    final_row(0)
    second(down0)
    final_row(1)
    finish_row(1)
    vectors, up_bias_grad, query_bias_grad, value_bias_grad = vector_grads()
    whole_result = join(results)
    second(attend0)
    third(up0)
    whole_grad = join(inputs_grad)
    third(down0)
    third(attend0)
    found1 = [(bulk, index * hidden_half) for index in range(3)]
    up_grad, down_grad = assemble([[up0, down0], found1[:2]], ("up", "down"), hidden_half)
    q_grad, k_grad, v_grad, o_grad = assemble(
        [[attend0], found1[2:]], ("query", "key", "value", "out"), heads_half
    )
    return (
        whole_result,
        whole_grad,
        vectors[:, 0],
        vectors[:, 1],
        q_grad,
        k_grad,
        v_grad,
        query_bias_grad,
        value_bias_grad,
        o_grad,
        vectors[:, 2],
        vectors[:, 3],
        vectors[:, 4],
        vectors[:, 5],
        up_grad,
        up_bias_grad,
        down_grad,
        vectors[:, 6],
        vectors[:, 7],
    )


def solution(mesh):
    split = Mesh(mesh.devices.reshape(mesh.shape[DP], 2, 2), (DP,) + SHARED)
    return jax.shard_map(
        functools.partial(per_device, mesh.shape[DP]),
        mesh=split,
        in_specs=(
            P(DP, None, None),
            P(DP, None),
            P(),
            P(),
            P(None, None, SHARED),
            P(None, None, SHARED),
            P(None, None, SHARED),
            P(None, SHARED),
            P(None, SHARED),
            P(None, None, SHARED),
            P(),
            P(),
            P(),
            P(),
            P(None, None, SHARED),
            P(None, SHARED),
            P(None, None, SHARED),
            P(),
            P(),
            P(DP, None, None),
        ),
        out_specs=(
            P(DP, None, None),
            P(DP, None, None),
            P(None, DP),
            P(None, DP),
            P(None, DP, SHARED),
            P(None, DP, SHARED),
            P(None, DP, SHARED),
            P(None, SHARED + (DP,)),
            P(None, SHARED + (DP,)),
            P(None, DP, SHARED),
            P(None, DP),
            P(None, DP),
            P(None, DP),
            P(None, DP),
            P(None, DP, SHARED),
            P(None, SHARED + (DP,)),
            P(None, DP, SHARED),
            P(None, DP),
            P(None, DP),
        ),
        check_vma=False,
    )
```

```python
import functools
import math

import jax
import jax.numpy as jnp
from jax import lax
from jax.experimental import pallas as pl
from jax.experimental.pallas import tpu as pltpu
from jax.sharding import Mesh
from jax.sharding import PartitionSpec as P

HD = 64
EPSILON = 1e-06
MASKED = -1e30
F32 = jnp.float32
BF16 = jnp.bfloat16
CONTRACT_LAST = (((1,), (1,)), ((), ()))
CONTRACT_ROWS = (((0,), (0,)), ((), ()))
MIB = 1024 * 1024
MICROSECOND = 3_690_000
SAMPLE = 2
SMALL = 32
DP, X, CORE = "dp", "x", "core"
SHARED = (X, CORE)
FAR, OUT, FUNC = "_hbm", "_out", "func"
BLOCK = 256


def dot(a, b):
    return jnp.dot(a, b, preferred_element_type=F32)


def dot_last(a, b):
    return lax.dot_general(a, b, CONTRACT_LAST, preferred_element_type=F32)


def dot_rows(a, b):
    return lax.dot_general(a, b, CONTRACT_ROWS, preferred_element_type=F32)


def normalise(values):
    center = values - jnp.mean(values, axis=-1, keepdims=True)
    spread = jnp.mean(center * center, axis=-1, keepdims=True)
    factor = lax.rsqrt(spread + EPSILON)
    return center * factor, factor


def norm_back(hat, factor, gain, grad):
    inner = grad * gain
    first = jnp.mean(inner, axis=-1, keepdims=True)
    second = jnp.mean(inner * hat, axis=-1, keepdims=True)
    return factor * (inner - first - hat * second)


def column_sum(values):
    return jnp.sum(values, axis=0, keepdims=True)


def both(mine, theirs):
    return mine[...].astype(F32) + theirs[...].astype(F32)


def sides(pair, first, axis):
    zero = jnp.zeros_like(pair)
    return jnp.concatenate([jnp.where(first, pair, zero), jnp.where(first, zero, pair)], axis=axis)


def term(*numbers):
    return "t" + "_".join(map(str, numbers))


class Refs:
    def __init__(self, names, refs):
        self.__dict__.update(zip(names, refs))
        self.names = {id(ref): name for name, ref in zip(names, refs)}
        self.loading, self.saving = {}, []

    def load(self, plan):
        for index, (name, target, part, place) in enumerate(plan):
            source = getattr(self, name)
            room = getattr(self, target)
            copy = pltpu.make_async_copy(
                source if part is None else source.at[part],
                room if place is None else room.at[place],
                self.load_sems.at[index],
            )
            copy.start()
            self.loading.setdefault(target, []).append(copy)

    def numbered(self, kind):
        found = []
        while hasattr(self, term(kind, len(found))):
            found.append(getattr(self, term(kind, len(found))))
        return found

    def need(self, *refs):
        for ref in refs:
            for copy in self.loading.pop(self.names[id(ref)], ()):
                copy.wait()

    def save(self, source, part=None):
        target = self.__dict__.get(self.names[id(source)] + OUT)
        if target is None:
            return
        if part is not None:
            source, target = source.at[part], target.at[part]
        copy = pltpu.make_async_copy(source, target, self.save_sems.at[len(self.saving)])
        copy.start()
        self.saving.append(copy)

    def finish(self):
        for name in list(self.loading):
            self.need(getattr(self, name))
        for copy in self.saving:
            copy.wait()


INSIDE = pl.BlockSpec(memory_space=pltpu.VMEM)
OUTSIDE = pl.BlockSpec(memory_space=pltpu.HBM)
SCALARS = pl.BlockSpec(memory_space=pltpu.SMEM)


class Chain:
    def __init__(self):
        self.mark = None


def title(body):
    while hasattr(body, FUNC):
        body = getattr(body, FUNC)
    return body.__name__


def run(chain, body, cost, near, far, inner, saved, room, table=None, limit=16, whole={}, over=None):
    names, values, in_specs = [], [], []
    if table is not None:
        names.append("table")
        values.append(table)
        in_specs.append(SCALARS)
    for key, value in near.items():
        names.append(key)
        values.append(pltpu.with_memory_space_constraint(value, pltpu.VMEM))
        in_specs.append(INSIDE)
    for key, value in far.items():
        names.append(key)
        values.append(pltpu.with_memory_space_constraint(value, pltpu.HBM))
        in_specs.append(OUTSIDE)
    aliases = {}
    if over is not None:
        aliases = {len(values): len(inner) + len(saved)}
        names.append("over")
        values.append(pltpu.with_memory_space_constraint(over, pltpu.HBM))
        in_specs.append(OUTSIDE)
    if chain.mark is not None:
        names.append("mark_in")
        values.append(chain.mark)
        in_specs.append(pl.BlockSpec(memory_space=pl.ANY))
    out_shape, out_specs = [], []
    for key, (shape, kind) in inner.items():
        names.append(key)
        out_shape.append(pltpu.VMEM(shape, kind))
        out_specs.append(INSIDE)
    for key, (shape, kind) in saved.items():
        names.append(key + OUT)
        out_shape.append(pltpu.HBM(shape, kind))
        out_specs.append(OUTSIDE)
    for key, (shape, kind) in whole.items():
        names.append(key + OUT)
        out_shape.append(pltpu.HBM(shape, kind))
        out_specs.append(OUTSIDE)
    names.append("mark")
    out_shape.append(jax.ShapeDtypeStruct((8, 128), F32))
    out_specs.append(pl.BlockSpec(memory_space=pl.ANY))
    scratch = []
    for key, (shape, kind) in {**saved, **room}.items():
        names.append(key)
        scratch.append(pltpu.VMEM(shape, kind))
    names += ["load_sems", "save_sems"]
    scratch += [pltpu.SemaphoreType.DMA((32,)), pltpu.SemaphoreType.DMA((32,))]

    def kernel(*refs):
        body(Refs(names, refs))

    outs = pl.pallas_call(
        kernel,
        out_shape=out_shape,
        in_specs=in_specs,
        out_specs=out_specs,
        scratch_shapes=scratch,
        input_output_aliases=aliases,
        compiler_params=pltpu.CompilerParams(vmem_limit_bytes=limit * MIB),
        cost_estimate=pl.CostEstimate(flops=1, bytes_accessed=cost * MICROSECOND, transcendentals=0),
        name=title(body),
    )(*values)
    chain.mark = outs[-1]
    return dict(zip([*inner, *saved, *whole], outs))


def stage(layer, names, r):
    plan = []
    for owner, target in (("_own", "w"), ("_other", "x")):
        at = 0
        for name in names:
            width = getattr(r, name + owner).shape[2]
            plan.append((name + owner, target, layer, (slice(None), slice(at, at + width))))
            at += width
    r.load(plan)
    r.finish()


def piece(r, side, index):
    return (r.w, r.x)[side][:, index * BLOCK : (index + 1) * BLOCK]


def attend_forward(layer, r):
    now = slice(layer, layer + 1)
    half = r.query.shape[1] // 2
    if layer == 0:
        values = r.source[...].astype(F32)
    else:
        last = slice(layer - 1, layer)
        fed = both(r.mine, r.theirs)
        values = r.middle[...] + r.feed_scale[last] * (fed + r.down_bias[last])
        r.fed[...] = fed.astype(BF16)
        r.save(r.fed)
    r.current[...] = values
    hat, factor = normalise(values)
    r.factor[...] = jnp.broadcast_to(factor, r.factor.shape)
    r.save(r.factor)
    normed = (hat * r.gain[now] + r.shift[now]).astype(BF16)
    r.normed[...] = normed
    r.save(r.normed)
    tokens = values.shape[0]
    for index, (target, bias) in enumerate(
        ((r.query, r.query_bias), (r.key, None), (r.value, r.value_bias))
    ):
        for side in range(2):
            cols = slice(side * half, (side + 1) * half)
            found = dot(normed, piece(r, side, index))
            if bias is not None:
                found = found + bias[now, cols]
            target[:, cols] = found.astype(BF16)
    r.save(r.query)
    r.save(r.key)
    r.save(r.value)
    lane = lax.broadcasted_iota(jnp.int32, (tokens, 2 * HD), 1)
    first = lane < HD
    scale = jnp.asarray(HD ** (-0.5), BF16)
    blocked = jnp.concatenate([r.mask[...], r.mask[...]], axis=0)
    for pair in range(half // HD):
        cols = slice(pair * 2 * HD, (pair + 1) * 2 * HD)
        scores = dot_last(sides(r.query[:, cols] * scale, first, 0), r.key[:, cols]) + blocked
        top = jnp.max(scores, axis=-1, keepdims=True)
        weights = jnp.exp(scores - top)
        total = jnp.sum(weights, axis=-1, keepdims=True)
        probs = (weights * (1.0 / total)).astype(BF16)
        r.probs[2 * pair] = probs[:tokens]
        r.probs[2 * pair + 1] = probs[tokens:]
        r.save(r.probs, slice(2 * pair, 2 * pair + 2))
        flat = jnp.concatenate([probs[:tokens], probs[tokens:]], axis=1)
        r.mixed[:, cols] = dot(flat, sides(r.value[:, cols], first, 0)).astype(BF16)
    r.save(r.mixed)
    contract(r, r.mixed, slice(3 * half, 4 * half), r.part)
    r.finish()


def contract(r, left, lanes, target):
    for start in range(0, target.shape[1], BLOCK):
        rows = slice(start, start + BLOCK)
        right = jnp.concatenate([r.w[rows, lanes], r.x[rows, lanes]], axis=1)
        target[:, rows] = dot_last(left[...], right).astype(BF16)


def block_of(r, index, start):
    half = r.w.shape[1] // 2
    return piece(r, start // half, (index * half + start % half) // BLOCK)


def half_of(r, index):
    half = r.w.shape[1] // 2
    return slice(index * half, (index + 1) * half)


def feed_enter(layer, r):
    now = slice(layer, layer + 1)
    attended = both(r.mine, r.theirs)
    values = r.current[...] + r.attend_scale[now] * (attended + r.out_bias[now])
    r.middle[...] = values
    r.save(r.middle)
    r.att[...] = attended.astype(BF16)
    r.save(r.att)
    hat, factor = normalise(values)
    r.factor2[...] = jnp.broadcast_to(factor, r.factor2.shape)
    r.save(r.factor2)
    normed = (hat * r.gain[now] + r.shift[now]).astype(BF16)
    r.normed2[...] = normed
    r.save(r.normed2)
    return normed


def expand(layer, r, normed, cols):
    before = dot(normed, block_of(r, 0, cols.start)) + r.up_bias[layer : layer + 1, cols]
    lower = 0.5 + 0.5 * lax.erf(before * math.sqrt(0.5))
    bell = jnp.exp(-0.5 * before * before) * (1.0 / math.sqrt(2.0 * math.pi))
    return (before * lower).astype(BF16), lower + before * bell


def feed_forward(layer, r):
    normed = feed_enter(layer, r)
    for start in range(0, r.act.shape[1], BLOCK):
        cols = slice(start, start + BLOCK)
        active, slope = expand(layer, r, normed, cols)
        r.act[:, cols] = active
        r.save(r.act, (slice(None), cols))
        r.slope[:, cols] = slope.astype(BF16)
        r.save(r.slope, (slice(None), cols))
    contract(r, r.act, half_of(r, 1), r.part)
    r.finish()


def feed_both(layer, r):
    now = slice(layer, layer + 1)
    scaled = r.feed_scale[now] * r.grad[...].astype(F32)
    grad_fed = scaled.astype(BF16)
    r.grad_fed[...] = grad_fed
    r.save(r.grad_fed)
    r.sums[...] = column_sum(scaled)
    normed = feed_enter(layer, r)
    for start in range(0, r.act.shape[1], BLOCK):
        cols = slice(start, start + BLOCK)
        active, slope = expand(layer, r, normed, cols)
        r.act[:, cols] = active
        r.save(r.act, (slice(None), cols))
        before = (dot(grad_fed, block_of(r, 1, start)) * slope).astype(BF16)
        r.before[:, cols] = before
        r.save(r.before, (slice(None), cols))
        r.wide_sums[:, cols] = column_sum(before.astype(F32))
    contract(r, r.act, half_of(r, 1), r.fed_part)
    r.save(r.fed_part)
    contract(r, r.before, half_of(r, 0), r.part)
    r.finish()


def finish_forward(layer, r):
    now = slice(layer, layer + 1)
    r.need(r.mine, r.theirs)
    fed = both(r.mine, r.theirs) + r.down_bias[now]
    r.need(r.middle)
    r.result[...] = (r.middle[...] + r.feed_scale[now] * fed).astype(BF16)
    r.save(r.result)
    r.sums[...] = column_sum(r.grad[...].astype(F32) * fed)
    r.finish()


def norm_enter(r, normed, factor, gain, shift):
    grad_normed = both(r.mine, r.theirs)
    hat = (normed[...].astype(F32) - shift) * (1.0 / gain)
    grad = norm_back(hat, factor[:, 0:1], gain, grad_normed)
    return grad, column_sum(grad_normed * hat), column_sum(grad_normed)


def feed_backward(layer, r):
    now = slice(layer, layer + 1)
    deep = slice(layer + 1, layer + 2)
    r.need(r.normed, r.factor)
    step, gain_sum, shift_sum = norm_enter(r, r.normed, r.factor, r.gain[deep], r.shift[deep])
    r.need(r.after)
    grad = r.after[...] + step
    r.grad[...] = grad
    r.save(r.grad)
    scaled = r.feed_scale[now] * grad
    grad_fed = scaled.astype(BF16)
    r.grad_fed[...] = grad_fed
    r.save(r.grad_fed)
    r.need(r.fed, r.slope)
    r.sums[0:1] = column_sum(scaled)
    r.sums[1:2] = column_sum(grad * (r.fed[...].astype(F32) + r.down_bias[now]))
    r.sums[2:3] = gain_sum
    r.sums[3:4] = shift_sum
    for start in range(0, r.before.shape[1], BLOCK):
        cols = slice(start, start + BLOCK)
        grad_active = dot(grad_fed, block_of(r, 1, start))
        before = (grad_active * r.slope[:, cols].astype(F32)).astype(BF16)
        r.before[:, cols] = before
        r.save(r.before, (slice(None), cols))
        r.wide_sums[:, cols] = column_sum(before.astype(F32))
    contract(r, r.before, half_of(r, 0), r.part)
    r.finish()


def attend_backward(layer, r):
    now = slice(layer, layer + 1)
    half = r.gq.shape[1] // 2
    r.need(r.normed2, r.factor2)
    step, gain_sum, shift_sum = norm_enter(r, r.normed2, r.factor2, r.gain[now], r.shift[now])
    r.need(r.grad)
    grad = r.grad[...].astype(F32) + step
    r.grad_middle[...] = grad
    r.save(r.grad_middle)
    scaled = r.attend_scale[now] * grad
    grad_att = scaled.astype(BF16)
    r.grad_att[...] = grad_att
    r.save(r.grad_att)
    r.need(r.att)
    r.sums[0:1] = column_sum(scaled)
    r.sums[1:2] = column_sum(grad * (r.att[...].astype(F32) + r.out_bias[now]))
    r.sums[2:3] = gain_sum
    r.sums[3:4] = shift_sum
    for side in range(2):
        cols = slice(side * half, (side + 1) * half)
        r.grad_mixed[:, cols] = dot(grad_att, piece(r, side, 3)).astype(BF16)
    r.need(r.value, r.probs, r.key, r.query)
    tokens = grad.shape[0]
    lane = lax.broadcasted_iota(jnp.int32, (tokens, 2 * HD), 1)
    first = lane < HD
    scale = HD ** (-0.5)
    for pair in range(half // HD):
        cols = slice(pair * 2 * HD, (pair + 1) * 2 * HD)
        mixed = sides(r.grad_mixed[:, cols], first, 0)
        probs_low = jnp.concatenate([r.probs[2 * pair], r.probs[2 * pair + 1]], axis=0)
        grad_probs = dot_last(mixed, r.value[:, cols])
        probs = probs_low.astype(F32)
        weighted = probs * grad_probs
        row = jnp.sum(weighted, axis=-1, keepdims=True)
        grad_scores = (weighted - probs * row).astype(BF16)
        flat = jnp.concatenate([grad_scores[:tokens], grad_scores[tokens:]], axis=1)
        r.gq[:, cols] = (dot(flat, sides(r.key[:, cols], first, 0)) * scale).astype(BF16)
        r.gk[:, cols] = (dot_rows(grad_scores, sides(r.query[:, cols], first, 0)) * scale).astype(
            BF16
        )
        r.gv[:, cols] = dot_rows(probs_low, mixed).astype(BF16)
    r.save(r.gq)
    r.save(r.gk)
    r.save(r.gv)
    r.wide_sums[0:1] = column_sum(r.gq[...].astype(F32))
    r.wide_sums[1:2] = column_sum(r.gv[...].astype(F32))
    left = [
        grad_now[:, side * half : (side + 1) * half]
        for side in range(2)
        for grad_now in (r.gq, r.gk, r.gv)
    ]
    left = jnp.concatenate(left, axis=1)
    for start in range(0, r.part.shape[1], BLOCK):
        cols = slice(start, start + BLOCK)
        right = jnp.concatenate([r.w[cols, : 3 * half], r.x[cols, : 3 * half]], axis=1)
        r.part[:, cols] = dot_last(left, right).astype(BF16)
    r.finish()


def finish_backward(r):
    r.need(r.normed, r.factor)
    step, gain_sum, shift_sum = norm_enter(r, r.normed, r.factor, r.gain[0:1], r.shift[0:1])
    r.need(r.after)
    r.input_grad[...] = r.after[...] + step
    r.save(r.input_grad)
    r.sums[0:1] = gain_sum
    r.sums[1:2] = shift_sum
    r.finish()


def with_loads(body, plan):
    def loaded(r):
        r.load(plan)
        body(r)

    loaded.func = body
    return loaded


def simple_plan(names):
    return [(name + FAR, name, None, None) for name in names]


def weight_grad(chunks, ways, groups, column, r):
    rows = getattr(r, groups[0][0] + str(0)).shape[1] // chunks
    split = chunks // 2
    r.gives = r.numbered(0)
    copies = []
    for side in (1, 0):
        for step in range(0, chunks, 2):
            at = 0
            if column is not None:
                places = [[(step + index) * rows for index in range(2)]]
                target, base = r.block, (side * chunks + step) * rows
            else:
                places = [
                    [
                        pl.multiple_of(r.table[way * chunks + step + index] * rows, rows)
                        for index in range(2)
                    ]
                    for way in range(ways)
                ]
                if side == 0:
                    target, base = (r.own_send, r.own_keep)[step // split], step % split * rows
                else:
                    parts = len(r.gives)
                    index, base = divmod(step * rows, chunks * rows // parts)
                    target = r.gives[index]
            where = slice(base, base + 2 * rows)
            for left_name, rights in groups:
                r.need(*(getattr(r, left_name + str(m)) for m in range(SAMPLE)))
                lefts = [
                    jnp.concatenate(
                        [
                            jnp.concatenate(
                                [
                                    getattr(r, left_name + str(m))[:, pl.ds(place, rows)]
                                    for place in pair
                                ],
                                axis=1,
                            )
                            for m in range(SAMPLE)
                        ],
                        axis=0,
                    )
                    for pair in places
                ]
                for right_name in rights:
                    r.need(*(getattr(r, right_name + str(m)) for m in range(SAMPLE)))
                    half = getattr(r, right_name + str(0)).shape[1] // 2
                    for offset in range(0, half, BLOCK):
                        lanes = slice(side * half + offset, side * half + offset + BLOCK)
                        right = jnp.concatenate(
                            [getattr(r, right_name + str(m))[:, lanes] for m in range(SAMPLE)],
                            axis=0,
                        )
                        left = lefts[(at + offset) * len(lefts) // target.shape[1]]
                        target[where, at + offset : at + offset + BLOCK] = dot_rows(
                            left, right
                        ).astype(BF16)
                    at += half
            if column is None:
                r.save(target, where)
                continue
            owner = r.table[0] if side == 0 else 1 - r.table[0]
            first = pl.multiple_of((owner * chunks + step) * rows, 2 * rows)
            copy = pltpu.make_async_copy(
                target.at[where],
                r.bulk_out.at[pl.ds(first, 2 * rows), column : column + at],
                r.save_sems.at[len(copies)],
            )
            copy.start()
            copies.append(copy)
    for copy in copies:
        copy.wait()
    r.finish()


def add_send(r):
    at = 0
    height = r.own_send.shape[0]
    targets = r.numbered(1)
    width = targets[0].shape[1]
    for got in r.numbered(0):
        rows = slice(at, min(at + got.shape[0], height))
        at = rows.stop
        for way, target in enumerate(targets):
            cols = slice(way * width, (way + 1) * width)
            left, right = r.own_send.at[rows, cols], got.at[: rows.stop - rows.start, cols]
            target[rows] = both(left, right).astype(BF16)


def add_first(r):
    gots = r.numbered(0)
    r.need(r.own_keep, *gots)
    leaves = r.numbered(2)
    rows, width = leaves[0].shape
    for way, (leave, arrived) in enumerate(zip(leaves, r.numbered(1))):
        cols = slice(way * width, (way + 1) * width)
        for side in range(2):
            where = slice(side * rows, (side + 1) * rows)
            part = where if len(gots) == 1 else slice(0, rows)
            total = both(r.own_keep.at[where, cols], gots[side % len(gots)].at[part, cols])
            total = (total + arrived[where].astype(F32)).astype(BF16)
            if side == 0:
                leave[...] = total
            else:
                r.stay[:, cols] = total
    r.finish()


def add_second(r):
    rows = r.leave.shape[0]
    for way, arrived in enumerate(r.numbered(1)):
        width = arrived.shape[1]
        cols = slice(way * width, (way + 1) * width)
        for target, where in ((r.leave, slice(0, rows)), (r.stay, slice(rows, 2 * rows))):
            target[:, cols] = both(r.keep.at[where, cols], arrived.at[where]).astype(BF16)


def add_third(r):
    r.found[...] = both(r.keep, r.arrived)
    r.save(r.found)
    r.finish()


def add_last(layers, pieces, names, r):
    each = len(names) // pieces
    width = getattr(r, names[0]).shape[2]
    for layer in reversed(range(layers)):
        for piece in range(pieces):
            if layer > 0:
                found = getattr(r, term(layer, piece, 0))
                r.need(found)
                total = found[...].astype(F32)
            else:
                total = both(*(getattr(r, term(layer, piece, index)) for index in range(2)))
            for index, name in enumerate(names[piece * each : (piece + 1) * each]):
                getattr(r, name)[layer] = total[:, index * width : (index + 1) * width]
                r.save(getattr(r, name), layer)
    r.finish()


def add_halves(r):
    total = r.keep[...] + r.arrived[...]
    half = r.leave.shape[0]
    r.leave[...] = total[:half]
    r.stay[...] = total[half:]


def place_rows(r):
    core = r.table[0]
    copies = []
    for index in range(SAMPLE):
        for side, owner in enumerate((core, 1 - core)):
            copy = pltpu.make_async_copy(
                getattr(r, term(side, index)),
                r.whole_out.at[owner * SAMPLE + index],
                r.save_sems.at[len(copies)],
            )
            copy.start()
            copies.append(copy)
    for copy in copies:
        copy.wait()


def gather_small(layers, heads_half, hidden_half, r):
    slots, _, each = r.own.shape

    def total(*numbers):
        return sum(getattr(r, term(*numbers, m))[...] for m in range(SAMPLE))

    common, up, wide = [], [[], []], [[], []]
    for layer in range(layers):
        feed, attend = total(layer, 2), total(layer, 0)
        if layer == 0:
            first = total(layers, 0)
        else:
            first = total(layer - 1, 2)[2:4]
        if layer == layers - 1:
            feed = jnp.concatenate([feed, total(layers, 1)], axis=0)
        common += [first, attend, feed[0:2]]
        feed_wide, attend_wide = total(layer, 3), total(layer, 1)
        for side in range(2):
            up[side].append(feed_wide[:, side * hidden_half : (side + 1) * hidden_half])
            wide[side].append(attend_wide[:, side * heads_half : (side + 1) * heads_half])
    common = jnp.concatenate(common, axis=0)
    r.common[...] = common
    for side in range(2):
        r.up[...] = jnp.concatenate(up[side], axis=0)
        target = (r.own, r.give)[side]
        rows = jnp.concatenate(wide[side], axis=0)
        for slot in range(slots):
            place = pl.ds(pl.multiple_of(r.table[slot] * each, each), each)
            target[slot] = jnp.zeros_like(target[slot])
            target[slot, : 8 * layers] = r.common[:, place]
            target[slot, 8 * layers : 9 * layers] = r.up[:, place]
            for index in range(2 * layers):
                for part in range(heads_half // each):
                    at = 9 * layers + index * (heads_half // each) + part
                    target[slot, at : at + 1] = rows[
                        index : index + 1, part * each : (part + 1) * each
                    ]


def per_device(
    n,
    activations,
    segments,
    first_gain,
    first_shift,
    query_weight,
    key_weight,
    value_weight,
    query_bias,
    value_bias,
    out_weight,
    out_bias,
    attend_scale,
    second_gain,
    second_shift,
    up_weight,
    up_bias,
    down_weight,
    down_bias,
    feed_scale,
    cotangent,
):
    rows, slots, width = activations.shape
    layers = first_gain.shape[0]
    core = lax.axis_index(CORE)
    mine_rows = rows // 2
    tokens = slots
    assert mine_rows == SAMPLE
    heads_half = query_weight.shape[2]
    hidden_half = up_weight.shape[2]
    features = 2 * heads_half
    hidden = 2 * hidden_half
    heads = features // HD
    samples = range(SAMPLE)
    direct = n == 8

    def swap_core(value):
        return lax.ppermute(value, CORE, [(0, 1), (1, 0)])

    def swap_x(value):
        return lax.ppermute(value, X, [(0, 1), (1, 0)])

    biases = jnp.concatenate([query_bias, value_bias, up_bias], axis=1)
    own = dict(wq=query_weight, wk=key_weight, wv=value_weight, wo=out_weight)
    own.update(wu=up_weight, wd=down_weight)
    biases_other = swap_core(biases)
    chain = Chain()

    attend_names = ("wq", "wk", "wv", "wo")
    feed_names = ("wu", "wd")
    other = {name: swap_core(own[name]) for name in attend_names}
    held_back = [own[name] for name in feed_names]
    held_back, other, biases_other = lax.optimization_barrier((held_back, other, biases_other))
    other.update({name: swap_core(value) for name, value in zip(feed_names, held_back)})

    def staged(layer, names):
        far = {}
        for name in names:
            far[name + "_own"], far[name + "_other"] = own[name], other[name]
        total = sum(own[name].shape[2] for name in names)
        return run(
            chain,
            functools.partial(stage, layer, names),
            total // 400,
            {},
            far,
            {side: ((width, total), BF16) for side in "wx"},
            {},
            {},
            limit=2,
        )

    pieces = jnp.concatenate([biases, biases_other], axis=1)
    span = heads_half * 2 + hidden_half
    query_bias_all = jnp.concatenate([pieces[:, :heads_half], pieces[:, span : span + heads_half]], 1)
    value_bias_all = jnp.concatenate(
        [pieces[:, heads_half:features], pieces[:, span + heads_half : span + features]], 1
    )
    up_bias_all = jnp.concatenate([pieces[:, features:span], pieces[:, span + features :]], 1)

    def own_rows(value):
        start = (core * mine_rows,) + (0,) * (value.ndim - 1)
        return lax.dynamic_slice(value, start, (mine_rows,) + value.shape[1:])

    own_segments = own_rows(segments)
    same = own_segments[:, :, None] == own_segments[:, None, :]
    held = ("grad", "query", "key", "value", "probs", "normed2", "att", "factor2")
    held += ("act", "before", "grad_fed")
    masks = jnp.where(same, 0.0, MASKED).astype(F32)
    own_input = own_rows(activations)
    own_cotangent = own_rows(cotangent)

    act = ((tokens, width), BF16)
    state = ((tokens, width), F32)
    head = ((tokens, features), BF16)
    hid = ((tokens, hidden), BF16)
    column = ((tokens, 128), F32)
    probs_shape = ((heads, slots, slots), BF16)

    kept = [[None] * SAMPLE for _ in range(layers)]
    feed_sums = [[None] * SAMPLE for _ in range(layers)]
    for layer in range(layers):
        last = layer == layers - 1
        attend_weights = staged(layer, attend_names)
        for m in samples:
            near = dict(mask=masks[m], gain=first_gain, shift=first_shift)
            near.update(query_bias=query_bias_all, value_bias=value_bias_all)
            near.update(attend_weights)
            saved = dict(
                normed=act, query=head, key=head, value=head, probs=probs_shape, mixed=head
            )
            saved["factor"] = column
            if layer == 0:
                near["source"] = own_input[m]
            else:
                before = kept[layer - 1][m]
                near.update(middle=before["middle"], mine=before["fed_mine"])
                near.update(theirs=before["fed_theirs"], feed_scale=feed_scale, down_bias=down_bias)
                saved["fed"] = act
            inner = dict(current=state, part=act)
            if last:
                inner.update({name: saved.pop(name) for name in list(saved) if name in held})
            outs = run(
                chain,
                functools.partial(attend_forward, layer),
                6,
                near,
                {},
                inner,
                saved,
                {},
            )
            if layer > 0:
                before["fed"] = outs.pop("fed")
            kept[layer][m] = now = dict(outs)
            now["mine"], now["theirs"] = outs["part"], swap_x(outs["part"])
        feed_weights = staged(layer, feed_names)
        for m in samples:
            now = kept[layer][m]
            near = {name: now[name] for name in ("current", "mine", "theirs")}
            near.update(attend_scale=attend_scale, out_bias=out_bias, up_bias=up_bias_all)
            near.update(gain=second_gain, shift=second_shift)
            near.update(feed_weights)
            inner = dict(middle=state, part=act)
            saved = dict(normed2=act, att=act, factor2=column, act=hid)
            if not last:
                saved["slope"] = hid
                body = feed_forward
            else:
                near.update(grad=own_cotangent[m], feed_scale=feed_scale)
                del inner["middle"]
                inner.update(sums=((1, width), F32), wide_sums=((1, hidden), F32))
                saved.update(middle=state, fed_part=act, grad_fed=act, before=hid)
                inner.update({name: saved.pop(name) for name in list(saved) if name in held})
                body = feed_both
            outs = run(
                chain,
                functools.partial(body, layer),
                11 if last else 7,
                near,
                {},
                inner,
                saved,
                {},
            )
            now.update(outs)
            if not last:
                now["fed_mine"], now["fed_theirs"] = outs["part"], swap_x(outs["part"])
            else:
                now["mine"], now["theirs"] = outs["part"], swap_x(outs["part"])
                now["fed_mine"] = outs["fed_part"]
                now["grad"] = own_cotangent[m]
                feed_sums[layer][m] = (outs["sums"], outs["wide_sums"])

    me = lax.axis_index(DP)
    def order_of(bits):
        if not direct:
            return jnp.arange(8).astype(jnp.int32)
        a, b, c = bits
        keep = (b + c, b, c, 0)
        return (me ^ jnp.array([a + r for r in keep] + list(keep))).astype(jnp.int32)

    table = order_of((1, 2, 4))
    len_table = 8

    core_now = core.astype(jnp.int32).reshape(1)
    half_shape = ((width // 2, 4 * heads_half), BF16)
    assert hidden_half == 4 * heads_half

    def products(layer, groups, column=None, bulk=None, span=1, ways=((1, 2, 4),), parts=1):
        if not direct:
            ways = ways[:1]
        near, far, room, plan = {}, {}, {}, []
        for left, rights in groups:
            for name in [left, *rights]:
                for m in samples:
                    value = kept[layer][m][name]
                    if name in held and layer == layers - 1:
                        near[name + str(m)] = value
                    else:
                        far[name + FAR + str(m)] = value
                        room[name + str(m)] = (value.shape, BF16)
                        plan.append((name + FAR + str(m), name + str(m), None, None))
        if column is not None:
            return run(
                chain,
                with_loads(functools.partial(weight_grad, 8, 1, groups, column), plan),
                6,
                near,
                far,
                {},
                {},
                dict(room, block=((2 * width, 4 * heads_half), BF16)),
                table=core_now,
                whole=dict(bulk=((2 * width, span * hidden_half), BF16)),
                over=bulk,
            )["bulk"]
        outs = run(
            chain,
            with_loads(functools.partial(weight_grad, 8, len(ways), groups, None), plan),
            6,
            near,
            far,
            dict(own_send=half_shape),
            dict(
                {term(0, i): ((width // parts, 4 * heads_half), BF16) for i in range(parts)},
                own_keep=half_shape,
            ),
            room,
            table=jnp.concatenate([order_of(bits) for bits in ways]),
            limit=16,
        )
        outs["got"] = [swap_core(outs[term(0, i)]) for i in range(parts)]
        outs["ways"] = ways
        return outs

    quarter_shape = ((width // 4, 4 * heads_half), BF16)
    eighth_shape = ((width // 8, 4 * heads_half), BF16)

    def swap_dp(value, bit):
        return lax.ppermute(value, DP, [(i, i ^ bit) for i in range(n)])

    def depart(outs):
        total = run(
            chain,
            add_send,
            1,
            dict(
                {term(0, i): v for i, v in enumerate(outs["got"][: max(1, len(outs["got"]) // 2)])},
                own_send=outs["own_send"],
            ),
            {},
            {
                term(1, way): ((width // 2, 4 * heads_half // len(outs["ways"])), BF16)
                for way in range(len(outs["ways"]))
            },
            {},
            {},
            limit=4,
        )
        totals = [total[term(1, way)] for way in range(len(outs["ways"]))]
        if direct:
            totals = [swap_dp(value, bits[0]) for value, bits in zip(totals, outs["ways"])]
        outs["arrived"] = totals

    def second(outs):
        if not direct:
            return
        gots = outs["got"]
        late = gots[len(gots) // 2 :]
        far, loads, plan = dict(own_keep=outs["own_keep"]), dict(own_keep=half_shape), []
        for index, value in enumerate(late):
            far[term(0, index)] = value
            loads[term(0, index)] = ((width // 2 // len(late), 4 * heads_half), BF16)
        for name in far:
            part = slice(width // 2, width) if far[name].shape[0] == width else None
            plan.append((name + FAR, name, part, None))
        found = run(
            chain,
            with_loads(add_first, plan),
            2,
            {term(1, way): value for way, value in enumerate(outs["arrived"])},
            {name + FAR: value for name, value in far.items()},
            dict(
                {
                    term(2, way): ((width // 4, 4 * heads_half // len(outs["ways"])), BF16)
                    for way in range(len(outs["ways"]))
                },
                stay=quarter_shape,
            ),
            {},
            loads,
            limit=8,
        )
        outs["keep"] = found["stay"]
        outs["arrived"] = [
            swap_dp(found[term(2, way)], bits[1]) for way, bits in enumerate(outs["ways"])
        ]

    def third(outs):
        if not direct:
            return
        found = run(
            chain,
            add_second,
            1,
            dict(
                {term(1, way): value for way, value in enumerate(outs["arrived"])},
                keep=outs["keep"],
            ),
            {},
            dict(leave=eighth_shape, stay=eighth_shape),
            {},
            {},
            limit=4,
        )
        outs["keep"], outs["arrived"] = found["stay"], swap_dp(found["leave"], 4)

    def fourth(outs):
        if not direct:
            got = jnp.concatenate(outs["got"], axis=0)
            keep = outs["own_keep"].astype(F32) + got[width // 2 :].astype(F32)
            rows_now = jnp.concatenate([outs["arrived"][0].astype(F32), keep], axis=0)
            return lax.psum_scatter(rows_now, DP, scatter_dimension=0, tiled=True)
        return run(
            chain,
            add_third,
            1,
            dict(arrived=outs["arrived"], keep=outs["keep"]),
            {},
            {},
            dict(found=(eighth_shape[0], F32)),
            {},
            limit=4,
        )["found"]

    def assemble(found, names, each):
        if not direct:
            found[0] = [fourth(value) for value in found[0]]
            found[1] = [array[:, at : at + hidden_half].astype(F32) for array, at in found[1]]
            joined = jnp.stack([jnp.concatenate(pieces_now, axis=1) for pieces_now in found])
            return [joined[:, :, i * each : (i + 1) * each] for i in range(len(names))]
        near, far, loads, plan = {}, {}, {}, []
        for layer, pieces_now in enumerate(found):
            for piece_now, value in enumerate(pieces_now):
                if layer == 0:
                    near[term(layer, piece_now, 0)] = value["keep"]
                    near[term(layer, piece_now, 1)] = value["arrived"]
                    continue
                name = term(layer, piece_now, 0)
                array, column = value
                far[name + FAR] = array
                shape = (array.shape[0], hidden_half)
                loads[name] = (shape, BF16)
                part = (slice(None), slice(column, column + hidden_half))
                plan.append((name + FAR, name, part, None))
        outs = run(
            chain,
            with_loads(functools.partial(add_last, layers, len(found[0]), names), plan),
            3,
            near,
            far,
            {},
            {name: ((layers, eighth_shape[0][0], each), F32) for name in names},
            loads,
            limit=12,
        )
        return [outs[name] for name in names]

    up_group = [("normed2", ["before"])]
    down_group = [("grad_fed", ["act"])]
    attend_group = [("normed", ["gq", "gk", "gv"]), ("grad_att", ["mixed"])]
    attend_sums = [[None] * SAMPLE for _ in range(layers)]

    def back_feed(layer, m, weights):
        now, deep = kept[layer][m], kept[layer + 1][m]
        near = dict(mine=deep["mine"], theirs=deep["theirs"])
        near.update(gain=first_gain, shift=first_shift)
        near.update(feed_scale=feed_scale, down_bias=down_bias)
        near.update(weights)
        far = dict(normed_hbm=deep["normed"], factor_hbm=deep["factor"])
        far.update(after_hbm=deep["grad_middle"], fed_hbm=now["fed"], slope_hbm=now["slope"])
        loads = dict(normed=act, factor=column, after=state, fed=act, slope=hid)
        outs = run(
            chain,
            with_loads(
                functools.partial(feed_backward, layer),
                simple_plan(loads),
            ),
            8,
            near,
            far,
            dict(part=act, sums=((4, width), F32), wide_sums=((1, hidden), F32)),
            dict(grad=state, grad_fed=act, before=hid),
            loads,
        )
        now.update(outs)
        now["mine"], now["theirs"] = outs["part"], swap_x(outs["part"])
        feed_sums[layer][m] = (outs["sums"], outs["wide_sums"])

    def back_attend(layer, m, weights):
        now = kept[layer][m]
        near = dict(mine=now["mine"], theirs=now["theirs"])
        near.update(gain=second_gain, shift=second_shift)
        near.update(attend_scale=attend_scale, out_bias=out_bias)
        near.update(weights)
        far, loads = {}, {}
        sources = dict(normed2=act, factor2=column, grad=act if layer == layers - 1 else state)
        sources["att"] = act
        sources.update(value=head, probs=probs_shape, key=head, query=head)
        for name, shape in sources.items():
            if layer == layers - 1 and name in held:
                near[name] = now[name]
            else:
                far[name + FAR] = now[name]
                loads[name] = shape
        outs = run(
            chain,
            with_loads(
                functools.partial(attend_backward, layer),
                simple_plan(loads),
            ),
            7,
            near,
            far,
            dict(
                part=act,
                sums=((4, width), F32),
                wide_sums=((2, features), F32),
            ),
            dict(grad_middle=state, grad_att=act, gq=head, gk=head, gv=head),
            dict(loads, grad_mixed=head),
        )
        now.update(outs)
        now["mine"], now["theirs"] = outs["part"], swap_x(outs["part"])
        attend_sums[layer][m] = (outs["sums"], outs["wide_sums"])

    results, last_sums = [], []

    def finish_row(m):
        now = kept[layers - 1][m]
        mine, _ = lax.optimization_barrier((now["fed_mine"], kept[0][SAMPLE - 1]["grad_att"]))
        far = dict(mine_hbm=mine, theirs_hbm=swap_x(mine), middle_hbm=now["middle"])
        near = dict(grad=own_cotangent[m], feed_scale=feed_scale, down_bias=down_bias)
        outs = run(
            chain,
            with_loads(
                functools.partial(finish_forward, layers - 1),
                simple_plan(("mine", "theirs", "middle")),
            ),
            2,
            near,
            far,
            dict(result=act, sums=((1, width), F32)),
            {},
            dict(mine=act, theirs=act, middle=state),
        )
        results.append(outs["result"])
        last_sums.append(outs["sums"])


    inputs_grad, final_sums = [], []

    def final_row(m):
        now = kept[0][m]
        near = dict(mine=now["mine"], theirs=now["theirs"])
        near.update(gain=first_gain, shift=first_shift)
        loads = dict(normed=act, factor=column, after=state)
        now["after"] = now["grad_middle"]
        outs = run(
            chain,
            with_loads(
                finish_backward, simple_plan(loads)
            ),
            2,
            near,
            {name + FAR: now[name] for name in loads},
            dict(input_grad=state, sums=((2, width), F32)),
            {},
            loads,
        )
        inputs_grad.append(outs["input_grad"])
        final_sums.append(outs["sums"])

    def gather_vectors():
        near = {}
        for layer in range(layers):
            for m in samples:
                attend_rows, attend_wide = attend_sums[layer][m]
                feed_rows, feed_wide = feed_sums[layer][m]
                for index, value in enumerate((attend_rows, attend_wide, feed_rows, feed_wide)):
                    near[term(layer, index, m)] = value
        for m in samples:
            near[term(layers, 0, m)] = final_sums[m]
            near[term(layers, 1, m)] = last_sums[m]
        each = width // len_table
        small_shape = ((len_table, SMALL, each), F32)
        outs = run(
            chain,
            functools.partial(gather_small, layers, heads_half, hidden_half),
            1,
            near,
            {},
            dict(own=small_shape, give=small_shape),
            {},
            dict(common=((8 * layers, width), F32), up=((layers, hidden_half), F32)),
            table=table,
            limit=4,
        )
        return outs["own"], swap_core(outs["give"])

    def halve(keep, arrived, bit):
        if not direct:
            return keep, arrived
        rows_now = keep.shape[0] // 2
        shape = ((rows_now,) + keep.shape[1:], F32)
        found = run(
            chain,
            add_halves,
            1,
            dict(keep=keep, arrived=arrived),
            {},
            dict(leave=shape, stay=shape),
            {},
            {},
            limit=2,
        )
        return found["stay"], swap_dp(found["leave"], bit)

    def vector_grads(keep, arrived):
        each = width // len_table
        small = keep + arrived
        if direct:
            total = small[0]
            vectors = total[: 8 * layers].reshape(layers, 8, each)
            up_bias_grad = total[8 * layers : 9 * layers]
            wide = total[9 * layers :].reshape(-1)[: 4 * layers * each * 2]
        else:
            total = lax.psum(small, DP).transpose(1, 0, 2).reshape(SMALL, -1)
            mine = lax.dynamic_slice_in_dim(total, me * (width // n), width // n, 1)
            vectors = mine[: 8 * layers].reshape(layers, 8, width // n)
            up_bias_grad = mine[8 * layers : 9 * layers]
            wide = total[9 * layers :, :each].reshape(-1)[: 4 * layers * each * 2]
        wide = wide[: 2 * layers * heads_half].reshape(layers, 2, heads_half)
        wide = lax.dynamic_slice_in_dim(wide, me * (heads_half // n), heads_half // n, 2)
        query_bias_grad, value_bias_grad = wide[:, 0], wide[:, 1]
        return vectors, up_bias_grad, query_bias_grad, value_bias_grad

    def join(values):
        near = {term(0, m): values[m] for m in samples}
        near.update({term(1, m): swap_core(values[m]) for m in samples})
        return run(
            chain,
            place_rows,
            3,
            near,
            {},
            {},
            {},
            {},
            table=core_now,
            limit=2,
            whole=dict(whole=((rows, slots, width), values[0].dtype)),
        )["whole"]

    assert layers == 2
    bulk = products(1, up_group, 0, None, 2)
    bulk = products(1, down_group, hidden_half, bulk, 2)
    bulk = lax.psum_scatter(bulk, (CORE, DP), scatter_dimension=0, tiled=True)
    attend_weights1 = staged(1, attend_names)
    back_attend(1, 0, attend_weights1)
    back_attend(1, 1, attend_weights1)
    feed_weights0 = staged(0, feed_names)
    back_feed(0, 0, feed_weights0)
    back_feed(0, 1, feed_weights0)
    attend_weights0 = staged(0, attend_names)
    back_attend(0, 0, attend_weights0)
    back_attend(0, 1, attend_weights0)
    bulk_attend = products(1, attend_group, 0, None, 1)
    bulk_attend = lax.psum_scatter(bulk_attend, (CORE, DP), scatter_dimension=0, tiled=True)
    up0 = products(0, up_group, ways=((1, 2, 4),), parts=2)
    down0 = products(0, down_group, ways=((2, 1, 4),), parts=1)
    depart(up0)
    attend0 = products(0, attend_group, ways=((1, 2, 4),), parts=1)
    depart(down0)
    depart(attend0)
    second(up0)
    second(down0)
    final_row(0)
    final_row(1)
    finish_row(0)
    finish_row(1)
    small_keep, small_arrived = gather_vectors()
    third(up0)
    small_keep, small_arrived = halve(small_keep, small_arrived, 1)
    second(attend0)
    whole_grad = join(inputs_grad)
    third(down0)
    small_keep, small_arrived = halve(small_keep, small_arrived, 2)
    whole_result = join(results)
    third(attend0)
    found1 = [(bulk, 0), (bulk, hidden_half)]
    up_grad, down_grad = assemble([[up0, down0], found1], ("up", "down"), hidden_half)
    small_keep, small_arrived = halve(small_keep, small_arrived, 4)
    q_grad, k_grad, v_grad, o_grad = assemble(
        [[attend0], [(bulk_attend, 0)]], ("query", "key", "value", "out"), heads_half
    )
    vectors, up_bias_grad, query_bias_grad, value_bias_grad = vector_grads(
        small_keep, small_arrived
    )
    return (
        whole_result,
        whole_grad,
        vectors[:, 0],
        vectors[:, 1],
        q_grad,
        k_grad,
        v_grad,
        query_bias_grad,
        value_bias_grad,
        o_grad,
        vectors[:, 2],
        vectors[:, 3],
        vectors[:, 4],
        vectors[:, 5],
        up_grad,
        up_bias_grad,
        down_grad,
        vectors[:, 6],
        vectors[:, 7],
    )


def solution(mesh):
    split = Mesh(mesh.devices.reshape(mesh.shape[DP], 2, 2), (DP,) + SHARED)
    return jax.shard_map(
        functools.partial(per_device, mesh.shape[DP]),
        mesh=split,
        in_specs=(
            P(DP, None, None),
            P(DP, None),
            P(),
            P(),
            P(None, None, SHARED),
            P(None, None, SHARED),
            P(None, None, SHARED),
            P(None, SHARED),
            P(None, SHARED),
            P(None, None, SHARED),
            P(),
            P(),
            P(),
            P(),
            P(None, None, SHARED),
            P(None, SHARED),
            P(None, None, SHARED),
            P(),
            P(),
            P(DP, None, None),
        ),
        out_specs=(
            P(DP, None, None),
            P(DP, None, None),
            P(None, DP),
            P(None, DP),
            P(None, DP, SHARED),
            P(None, DP, SHARED),
            P(None, DP, SHARED),
            P(None, SHARED + (DP,)),
            P(None, SHARED + (DP,)),
            P(None, DP, SHARED),
            P(None, DP),
            P(None, DP),
            P(None, DP),
            P(None, DP),
            P(None, DP, SHARED),
            P(None, SHARED + (DP,)),
            P(None, DP, SHARED),
            P(None, DP),
            P(None, DP),
        ),
        check_vma=False,
    )
```

```python
import functools
import math

import jax
import jax.numpy as jnp
from jax import lax
from jax.experimental import pallas as pl
from jax.experimental.pallas import tpu as pltpu
from jax.sharding import Mesh
from jax.sharding import PartitionSpec as P

HD = 64
EPSILON = 1e-06
MASKED = -1e30
F32 = jnp.float32
BF16 = jnp.bfloat16
CONTRACT_LAST = (((1,), (1,)), ((), ()))
CONTRACT_ROWS = (((0,), (0,)), ((), ()))
MIB = 1024 * 1024
MICROSECOND = 3_690_000
SAMPLE = 2
SMALL = 32
DP, X, CORE = "dp", "x", "core"
SHARED = (X, CORE)
FAR, OUT, FUNC = "_hbm", "_out", "func"
BLOCK = 256


def dot(a, b):
    return jnp.dot(a, b, preferred_element_type=F32)


def dot_last(a, b):
    return lax.dot_general(a, b, CONTRACT_LAST, preferred_element_type=F32)


def dot_rows(a, b):
    return lax.dot_general(a, b, CONTRACT_ROWS, preferred_element_type=F32)


def normalise(values):
    center = values - jnp.mean(values, axis=-1, keepdims=True)
    spread = jnp.mean(center * center, axis=-1, keepdims=True)
    factor = lax.rsqrt(spread + EPSILON)
    return center * factor, factor


def norm_back(hat, factor, gain, grad):
    inner = grad * gain
    first = jnp.mean(inner, axis=-1, keepdims=True)
    second = jnp.mean(inner * hat, axis=-1, keepdims=True)
    return factor * (inner - first - hat * second)


def column_sum(values):
    return jnp.sum(values, axis=0, keepdims=True)


def both(mine, theirs):
    return mine[...].astype(F32) + theirs[...].astype(F32)


def sides(pair, first, axis):
    zero = jnp.zeros_like(pair)
    return jnp.concatenate([jnp.where(first, pair, zero), jnp.where(first, zero, pair)], axis=axis)


def term(*numbers):
    return "t" + "_".join(map(str, numbers))


class Refs:
    def __init__(self, names, refs):
        self.__dict__.update(zip(names, refs))
        self.names = {id(ref): name for name, ref in zip(names, refs)}
        self.loading, self.saving = {}, []

    def load(self, plan):
        for index, (name, target, part, place) in enumerate(plan):
            source = getattr(self, name)
            room = getattr(self, target)
            copy = pltpu.make_async_copy(
                source if part is None else source.at[part],
                room if place is None else room.at[place],
                self.load_sems.at[index],
            )
            copy.start()
            self.loading.setdefault(target, []).append(copy)

    def numbered(self, kind):
        found = []
        while hasattr(self, term(kind, len(found))):
            found.append(getattr(self, term(kind, len(found))))
        return found

    def need(self, *refs):
        for ref in refs:
            for copy in self.loading.pop(self.names[id(ref)], ()):
                copy.wait()

    def save(self, source, part=None):
        target = self.__dict__.get(self.names[id(source)] + OUT)
        if target is None:
            return
        if part is not None:
            source, target = source.at[part], target.at[part]
        copy = pltpu.make_async_copy(source, target, self.save_sems.at[len(self.saving)])
        copy.start()
        self.saving.append(copy)

    def finish(self):
        for name in list(self.loading):
            self.need(getattr(self, name))
        for copy in self.saving:
            copy.wait()


INSIDE = pl.BlockSpec(memory_space=pltpu.VMEM)
OUTSIDE = pl.BlockSpec(memory_space=pltpu.HBM)
SCALARS = pl.BlockSpec(memory_space=pltpu.SMEM)


class Chain:
    def __init__(self):
        self.mark = None


def title(body):
    while hasattr(body, FUNC):
        body = getattr(body, FUNC)
    return body.__name__


def run(chain, body, cost, near, far, inner, saved, room, table=None, limit=16, whole={}, over=None):
    names, values, in_specs = [], [], []
    if table is not None:
        names.append("table")
        values.append(table)
        in_specs.append(SCALARS)
    for key, value in near.items():
        names.append(key)
        values.append(pltpu.with_memory_space_constraint(value, pltpu.VMEM))
        in_specs.append(INSIDE)
    for key, value in far.items():
        names.append(key)
        values.append(pltpu.with_memory_space_constraint(value, pltpu.HBM))
        in_specs.append(OUTSIDE)
    aliases = {}
    if over is not None:
        aliases = {len(values): len(inner) + len(saved)}
        names.append("over")
        values.append(pltpu.with_memory_space_constraint(over, pltpu.HBM))
        in_specs.append(OUTSIDE)
    if chain.mark is not None:
        names.append("mark_in")
        values.append(chain.mark)
        in_specs.append(pl.BlockSpec(memory_space=pl.ANY))
    out_shape, out_specs = [], []
    for key, (shape, kind) in inner.items():
        names.append(key)
        out_shape.append(pltpu.VMEM(shape, kind))
        out_specs.append(INSIDE)
    for key, (shape, kind) in saved.items():
        names.append(key + OUT)
        out_shape.append(pltpu.HBM(shape, kind))
        out_specs.append(OUTSIDE)
    for key, (shape, kind) in whole.items():
        names.append(key + OUT)
        out_shape.append(pltpu.HBM(shape, kind))
        out_specs.append(OUTSIDE)
    names.append("mark")
    out_shape.append(jax.ShapeDtypeStruct((8, 128), F32))
    out_specs.append(pl.BlockSpec(memory_space=pl.ANY))
    scratch = []
    for key, (shape, kind) in {**saved, **room}.items():
        names.append(key)
        scratch.append(pltpu.VMEM(shape, kind))
    names += ["load_sems", "save_sems"]
    scratch += [pltpu.SemaphoreType.DMA((32,)), pltpu.SemaphoreType.DMA((32,))]

    def kernel(*refs):
        body(Refs(names, refs))

    outs = pl.pallas_call(
        kernel,
        out_shape=out_shape,
        in_specs=in_specs,
        out_specs=out_specs,
        scratch_shapes=scratch,
        input_output_aliases=aliases,
        compiler_params=pltpu.CompilerParams(vmem_limit_bytes=limit * MIB),
        cost_estimate=pl.CostEstimate(flops=1, bytes_accessed=cost * MICROSECOND, transcendentals=0),
        name=title(body),
    )(*values)
    chain.mark = outs[-1]
    return dict(zip([*inner, *saved, *whole], outs))


def stage(layer, names, r):
    plan = []
    for owner, target in (("_own", "w"), ("_other", "x")):
        at = 0
        for name in names:
            width = getattr(r, name + owner).shape[2]
            plan.append((name + owner, target, layer, (slice(None), slice(at, at + width))))
            at += width
    r.load(plan)
    r.finish()


def piece(r, side, index):
    return (r.w, r.x)[side][:, index * BLOCK : (index + 1) * BLOCK]


def attend_forward(layer, r):
    now = slice(layer, layer + 1)
    half = r.query.shape[1] // 2
    if layer == 0:
        values = r.source[...].astype(F32)
    else:
        last = slice(layer - 1, layer)
        fed = both(r.mine, r.theirs)
        values = r.middle[...] + r.feed_scale[last] * (fed + r.down_bias[last])
        r.fed[...] = fed.astype(BF16)
        r.save(r.fed)
    r.current[...] = values
    hat, factor = normalise(values)
    r.factor[...] = jnp.broadcast_to(factor, r.factor.shape)
    r.save(r.factor)
    normed = (hat * r.gain[now] + r.shift[now]).astype(BF16)
    r.normed[...] = normed
    r.save(r.normed)
    tokens = values.shape[0]
    for index, (target, bias) in enumerate(
        ((r.query, r.query_bias), (r.key, None), (r.value, r.value_bias))
    ):
        for side in range(2):
            cols = slice(side * half, (side + 1) * half)
            found = dot(normed, piece(r, side, index))
            if bias is not None:
                found = found + bias[now, cols]
            target[:, cols] = found.astype(BF16)
    r.save(r.query)
    r.save(r.key)
    r.save(r.value)
    lane = lax.broadcasted_iota(jnp.int32, (tokens, 2 * HD), 1)
    first = lane < HD
    scale = jnp.asarray(HD ** (-0.5), BF16)
    blocked = jnp.concatenate([r.mask[...], r.mask[...]], axis=0)
    for pair in range(half // HD):
        cols = slice(pair * 2 * HD, (pair + 1) * 2 * HD)
        scores = dot_last(sides(r.query[:, cols] * scale, first, 0), r.key[:, cols]) + blocked
        top = jnp.max(scores, axis=-1, keepdims=True)
        weights = jnp.exp(scores - top)
        total = jnp.sum(weights, axis=-1, keepdims=True)
        probs = (weights * (1.0 / total)).astype(BF16)
        r.probs[2 * pair] = probs[:tokens]
        r.probs[2 * pair + 1] = probs[tokens:]
        r.save(r.probs, slice(2 * pair, 2 * pair + 2))
        flat = jnp.concatenate([probs[:tokens], probs[tokens:]], axis=1)
        r.mixed[:, cols] = dot(flat, sides(r.value[:, cols], first, 0)).astype(BF16)
    r.save(r.mixed)
    contract(r, r.mixed, slice(3 * half, 4 * half), r.part)
    r.finish()


def contract(r, left, lanes, target):
    for start in range(0, target.shape[1], BLOCK):
        rows = slice(start, start + BLOCK)
        right = jnp.concatenate([r.w[rows, lanes], r.x[rows, lanes]], axis=1)
        target[:, rows] = dot_last(left[...], right).astype(BF16)


def block_of(r, index, start):
    half = r.w.shape[1] // 2
    return piece(r, start // half, (index * half + start % half) // BLOCK)


def half_of(r, index):
    half = r.w.shape[1] // 2
    return slice(index * half, (index + 1) * half)


def feed_enter(layer, r):
    now = slice(layer, layer + 1)
    attended = both(r.mine, r.theirs)
    values = r.current[...] + r.attend_scale[now] * (attended + r.out_bias[now])
    r.middle[...] = values
    r.save(r.middle)
    r.att[...] = attended.astype(BF16)
    r.save(r.att)
    hat, factor = normalise(values)
    r.factor2[...] = jnp.broadcast_to(factor, r.factor2.shape)
    r.save(r.factor2)
    normed = (hat * r.gain[now] + r.shift[now]).astype(BF16)
    r.normed2[...] = normed
    r.save(r.normed2)
    return normed


def expand(layer, r, normed, cols):
    before = dot(normed, block_of(r, 0, cols.start)) + r.up_bias[layer : layer + 1, cols]
    lower = 0.5 + 0.5 * lax.erf(before * math.sqrt(0.5))
    bell = jnp.exp(-0.5 * before * before) * (1.0 / math.sqrt(2.0 * math.pi))
    return (before * lower).astype(BF16), lower + before * bell


def feed_forward(layer, r):
    normed = feed_enter(layer, r)
    for start in range(0, r.act.shape[1], BLOCK):
        cols = slice(start, start + BLOCK)
        active, slope = expand(layer, r, normed, cols)
        r.act[:, cols] = active
        r.save(r.act, (slice(None), cols))
        r.slope[:, cols] = slope.astype(BF16)
        r.save(r.slope, (slice(None), cols))
    contract(r, r.act, half_of(r, 1), r.part)
    r.finish()


def feed_both(layer, r):
    now = slice(layer, layer + 1)
    scaled = r.feed_scale[now] * r.grad[...].astype(F32)
    grad_fed = scaled.astype(BF16)
    r.grad_fed[...] = grad_fed
    r.save(r.grad_fed)
    r.sums[...] = column_sum(scaled)
    normed = feed_enter(layer, r)
    for start in range(0, r.act.shape[1], BLOCK):
        cols = slice(start, start + BLOCK)
        active, slope = expand(layer, r, normed, cols)
        r.act[:, cols] = active
        r.save(r.act, (slice(None), cols))
        before = (dot(grad_fed, block_of(r, 1, start)) * slope).astype(BF16)
        r.before[:, cols] = before
        r.save(r.before, (slice(None), cols))
        r.wide_sums[:, cols] = column_sum(before.astype(F32))
    contract(r, r.act, half_of(r, 1), r.fed_part)
    r.save(r.fed_part)
    contract(r, r.before, half_of(r, 0), r.part)
    r.finish()


def finish_forward(layer, r):
    now = slice(layer, layer + 1)
    r.need(r.mine, r.theirs)
    fed = both(r.mine, r.theirs) + r.down_bias[now]
    r.need(r.middle)
    r.result[...] = (r.middle[...] + r.feed_scale[now] * fed).astype(BF16)
    r.save(r.result)
    r.sums[...] = column_sum(r.grad[...].astype(F32) * fed)
    r.finish()


def norm_enter(r, normed, factor, gain, shift):
    grad_normed = both(r.mine, r.theirs)
    hat = (normed[...].astype(F32) - shift) * (1.0 / gain)
    grad = norm_back(hat, factor[:, 0:1], gain, grad_normed)
    return grad, column_sum(grad_normed * hat), column_sum(grad_normed)


def feed_backward(layer, r):
    now = slice(layer, layer + 1)
    deep = slice(layer + 1, layer + 2)
    r.need(r.normed, r.factor)
    step, gain_sum, shift_sum = norm_enter(r, r.normed, r.factor, r.gain[deep], r.shift[deep])
    r.need(r.after)
    grad = r.after[...] + step
    r.grad[...] = grad
    r.save(r.grad)
    scaled = r.feed_scale[now] * grad
    grad_fed = scaled.astype(BF16)
    r.grad_fed[...] = grad_fed
    r.save(r.grad_fed)
    r.need(r.fed, r.slope)
    r.sums[0:1] = column_sum(scaled)
    r.sums[1:2] = column_sum(grad * (r.fed[...].astype(F32) + r.down_bias[now]))
    r.sums[2:3] = gain_sum
    r.sums[3:4] = shift_sum
    for start in range(0, r.before.shape[1], BLOCK):
        cols = slice(start, start + BLOCK)
        grad_active = dot(grad_fed, block_of(r, 1, start))
        before = (grad_active * r.slope[:, cols].astype(F32)).astype(BF16)
        r.before[:, cols] = before
        r.save(r.before, (slice(None), cols))
        r.wide_sums[:, cols] = column_sum(before.astype(F32))
    contract(r, r.before, half_of(r, 0), r.part)
    r.finish()


def attend_backward(layer, r):
    now = slice(layer, layer + 1)
    half = r.gq.shape[1] // 2
    r.need(r.normed2, r.factor2)
    step, gain_sum, shift_sum = norm_enter(r, r.normed2, r.factor2, r.gain[now], r.shift[now])
    r.need(r.grad)
    grad = r.grad[...].astype(F32) + step
    r.grad_middle[...] = grad
    r.save(r.grad_middle)
    scaled = r.attend_scale[now] * grad
    grad_att = scaled.astype(BF16)
    r.grad_att[...] = grad_att
    r.save(r.grad_att)
    r.need(r.att)
    r.sums[0:1] = column_sum(scaled)
    r.sums[1:2] = column_sum(grad * (r.att[...].astype(F32) + r.out_bias[now]))
    r.sums[2:3] = gain_sum
    r.sums[3:4] = shift_sum
    for side in range(2):
        cols = slice(side * half, (side + 1) * half)
        r.grad_mixed[:, cols] = dot(grad_att, piece(r, side, 3)).astype(BF16)
    r.need(r.value, r.probs, r.key, r.query)
    tokens = grad.shape[0]
    lane = lax.broadcasted_iota(jnp.int32, (tokens, 2 * HD), 1)
    first = lane < HD
    scale = HD ** (-0.5)
    for pair in range(half // HD):
        cols = slice(pair * 2 * HD, (pair + 1) * 2 * HD)
        mixed = sides(r.grad_mixed[:, cols], first, 0)
        probs_low = jnp.concatenate([r.probs[2 * pair], r.probs[2 * pair + 1]], axis=0)
        grad_probs = dot_last(mixed, r.value[:, cols])
        probs = probs_low.astype(F32)
        weighted = probs * grad_probs
        row = jnp.sum(weighted, axis=-1, keepdims=True)
        grad_scores = (weighted - probs * row).astype(BF16)
        flat = jnp.concatenate([grad_scores[:tokens], grad_scores[tokens:]], axis=1)
        r.gq[:, cols] = (dot(flat, sides(r.key[:, cols], first, 0)) * scale).astype(BF16)
        r.gk[:, cols] = (dot_rows(grad_scores, sides(r.query[:, cols], first, 0)) * scale).astype(
            BF16
        )
        r.gv[:, cols] = dot_rows(probs_low, mixed).astype(BF16)
    r.save(r.gq)
    r.save(r.gk)
    r.save(r.gv)
    r.wide_sums[0:1] = column_sum(r.gq[...].astype(F32))
    r.wide_sums[1:2] = column_sum(r.gv[...].astype(F32))
    left = [
        grad_now[:, side * half : (side + 1) * half]
        for side in range(2)
        for grad_now in (r.gq, r.gk, r.gv)
    ]
    left = jnp.concatenate(left, axis=1)
    for start in range(0, r.part.shape[1], BLOCK):
        cols = slice(start, start + BLOCK)
        right = jnp.concatenate([r.w[cols, : 3 * half], r.x[cols, : 3 * half]], axis=1)
        r.part[:, cols] = dot_last(left, right).astype(BF16)
    r.finish()


def finish_backward(r):
    r.need(r.normed, r.factor)
    step, gain_sum, shift_sum = norm_enter(r, r.normed, r.factor, r.gain[0:1], r.shift[0:1])
    r.need(r.after)
    r.input_grad[...] = r.after[...] + step
    r.save(r.input_grad)
    r.sums[0:1] = gain_sum
    r.sums[1:2] = shift_sum
    r.finish()


def with_loads(body, plan):
    def loaded(r):
        r.load(plan)
        body(r)

    loaded.func = body
    return loaded


def simple_plan(names):
    return [(name + FAR, name, None, None) for name in names]


def weight_grad(chunks, ways, groups, column, r):
    rows = getattr(r, groups[0][0] + str(0)).shape[1] // chunks
    split = chunks // 2
    r.gives = r.numbered(0)
    copies = []
    for side in (1, 0):
        for step in range(0, chunks, 2):
            at = 0
            if column is not None:
                places = [[(step + index) * rows for index in range(2)]]
                target, base = r.block, (side * chunks + step) * rows
            else:
                places = [
                    [
                        pl.multiple_of(r.table[way * chunks + step + index] * rows, rows)
                        for index in range(2)
                    ]
                    for way in range(ways)
                ]
                if side == 0:
                    target, base = (r.own_send, r.own_keep)[step // split], step % split * rows
                else:
                    parts = len(r.gives)
                    index, base = divmod(step * rows, chunks * rows // parts)
                    target = r.gives[index]
            where = slice(base, base + 2 * rows)
            for left_name, rights in groups:
                r.need(*(getattr(r, left_name + str(m)) for m in range(SAMPLE)))
                lefts = [
                    jnp.concatenate(
                        [
                            jnp.concatenate(
                                [
                                    getattr(r, left_name + str(m))[:, pl.ds(place, rows)]
                                    for place in pair
                                ],
                                axis=1,
                            )
                            for m in range(SAMPLE)
                        ],
                        axis=0,
                    )
                    for pair in places
                ]
                for right_name in rights:
                    r.need(*(getattr(r, right_name + str(m)) for m in range(SAMPLE)))
                    half = getattr(r, right_name + str(0)).shape[1] // 2
                    for offset in range(0, half, BLOCK):
                        lanes = slice(side * half + offset, side * half + offset + BLOCK)
                        right = jnp.concatenate(
                            [getattr(r, right_name + str(m))[:, lanes] for m in range(SAMPLE)],
                            axis=0,
                        )
                        left = lefts[(at + offset) * len(lefts) // target.shape[1]]
                        target[where, at + offset : at + offset + BLOCK] = dot_rows(
                            left, right
                        ).astype(BF16)
                    at += half
            if column is None:
                r.save(target, where)
                continue
            owner = r.table[0] if side == 0 else 1 - r.table[0]
            first = pl.multiple_of((owner * chunks + step) * rows, 2 * rows)
            copy = pltpu.make_async_copy(
                target.at[where],
                r.bulk_out.at[pl.ds(first, 2 * rows), column : column + at],
                r.save_sems.at[len(copies)],
            )
            copy.start()
            copies.append(copy)
    for copy in copies:
        copy.wait()
    r.finish()


def add_send(r):
    at = 0
    height = r.own_send.shape[0]
    targets = r.numbered(1)
    width = targets[0].shape[1]
    for got in r.numbered(0):
        rows = slice(at, min(at + got.shape[0], height))
        at = rows.stop
        for way, target in enumerate(targets):
            cols = slice(way * width, (way + 1) * width)
            left, right = r.own_send.at[rows, cols], got.at[: rows.stop - rows.start, cols]
            target[rows] = both(left, right).astype(BF16)


def add_first(r):
    gots = r.numbered(0)
    r.need(r.own_keep, *gots)
    leaves = r.numbered(2)
    rows, width = leaves[0].shape
    for way, (leave, arrived) in enumerate(zip(leaves, r.numbered(1))):
        cols = slice(way * width, (way + 1) * width)
        for side in range(2):
            where = slice(side * rows, (side + 1) * rows)
            part = where if len(gots) == 1 else slice(0, rows)
            total = both(r.own_keep.at[where, cols], gots[side % len(gots)].at[part, cols])
            total = (total + arrived[where].astype(F32)).astype(BF16)
            if side == 0:
                leave[...] = total
            else:
                r.stay[:, cols] = total
    r.finish()


def add_second(r):
    rows = r.leave.shape[0]
    for way, arrived in enumerate(r.numbered(1)):
        width = arrived.shape[1]
        cols = slice(way * width, (way + 1) * width)
        for target, where in ((r.leave, slice(0, rows)), (r.stay, slice(rows, 2 * rows))):
            target[:, cols] = both(r.keep.at[where, cols], arrived.at[where]).astype(BF16)


def add_third(r):
    r.found[...] = both(r.keep, r.arrived)
    r.save(r.found)
    r.finish()


def add_last(layers, pieces, names, r):
    each = len(names) // pieces
    width = getattr(r, names[0]).shape[2]
    for layer in reversed(range(layers)):
        for piece in range(pieces):
            if layer > 0:
                found = getattr(r, term(layer, piece, 0))
                r.need(found)
                total = found[...].astype(F32)
            else:
                total = both(*(getattr(r, term(layer, piece, index)) for index in range(2)))
            for index, name in enumerate(names[piece * each : (piece + 1) * each]):
                getattr(r, name)[layer] = total[:, index * width : (index + 1) * width]
                r.save(getattr(r, name), layer)
    r.finish()


def add_halves(r):
    total = r.keep[...] + r.arrived[...]
    half = r.leave.shape[0]
    r.leave[...] = total[:half]
    r.stay[...] = total[half:]


def place_rows(r):
    core = r.table[0]
    copies = []
    for index in range(SAMPLE):
        for side, owner in enumerate((core, 1 - core)):
            copy = pltpu.make_async_copy(
                getattr(r, term(side, index)),
                r.whole_out.at[owner * SAMPLE + index],
                r.save_sems.at[len(copies)],
            )
            copy.start()
            copies.append(copy)
    for copy in copies:
        copy.wait()


def gather_small(layers, heads_half, hidden_half, r):
    slots, _, each = r.own.shape

    def total(*numbers):
        return sum(getattr(r, term(*numbers, m))[...] for m in range(SAMPLE))

    common, up, wide = [], [[], []], [[], []]
    for layer in range(layers):
        feed, attend = total(layer, 2), total(layer, 0)
        if layer == 0:
            first = total(layers, 0)
        else:
            first = total(layer - 1, 2)[2:4]
        if layer == layers - 1:
            feed = jnp.concatenate([feed, total(layers, 1)], axis=0)
        common += [first, attend, feed[0:2]]
        feed_wide, attend_wide = total(layer, 3), total(layer, 1)
        for side in range(2):
            up[side].append(feed_wide[:, side * hidden_half : (side + 1) * hidden_half])
            wide[side].append(attend_wide[:, side * heads_half : (side + 1) * heads_half])
    common = jnp.concatenate(common, axis=0)
    r.common[...] = common
    for side in range(2):
        r.up[...] = jnp.concatenate(up[side], axis=0)
        target = (r.own, r.give)[side]
        rows = jnp.concatenate(wide[side], axis=0)
        for slot in range(slots):
            place = pl.ds(pl.multiple_of(r.table[slot] * each, each), each)
            target[slot] = jnp.zeros_like(target[slot])
            target[slot, : 8 * layers] = r.common[:, place]
            target[slot, 8 * layers : 9 * layers] = r.up[:, place]
            for index in range(2 * layers):
                for part in range(heads_half // each):
                    at = 9 * layers + index * (heads_half // each) + part
                    target[slot, at : at + 1] = rows[
                        index : index + 1, part * each : (part + 1) * each
                    ]


def per_device(
    n,
    activations,
    segments,
    first_gain,
    first_shift,
    query_weight,
    key_weight,
    value_weight,
    query_bias,
    value_bias,
    out_weight,
    out_bias,
    attend_scale,
    second_gain,
    second_shift,
    up_weight,
    up_bias,
    down_weight,
    down_bias,
    feed_scale,
    cotangent,
):
    rows, slots, width = activations.shape
    layers = first_gain.shape[0]
    core = lax.axis_index(CORE)
    mine_rows = rows // 2
    tokens = slots
    assert mine_rows == SAMPLE
    heads_half = query_weight.shape[2]
    hidden_half = up_weight.shape[2]
    features = 2 * heads_half
    hidden = 2 * hidden_half
    heads = features // HD
    samples = range(SAMPLE)
    direct = n == 8

    def swap_core(value):
        return lax.ppermute(value, CORE, [(0, 1), (1, 0)])

    def swap_x(value):
        return lax.ppermute(value, X, [(0, 1), (1, 0)])

    biases = jnp.concatenate([query_bias, value_bias, up_bias], axis=1)
    own = dict(wq=query_weight, wk=key_weight, wv=value_weight, wo=out_weight)
    own.update(wu=up_weight, wd=down_weight)
    biases_other = swap_core(biases)
    chain = Chain()

    attend_names = ("wq", "wk", "wv", "wo")
    feed_names = ("wu", "wd")
    other = {name: swap_core(own[name]) for name in attend_names}
    held_back = [own[name] for name in feed_names]
    held_back, other, biases_other = lax.optimization_barrier((held_back, other, biases_other))
    other.update({name: swap_core(value) for name, value in zip(feed_names, held_back)})

    def staged(layer, names):
        far = {}
        for name in names:
            far[name + "_own"], far[name + "_other"] = own[name], other[name]
        total = sum(own[name].shape[2] for name in names)
        return run(
            chain,
            functools.partial(stage, layer, names),
            total // 400,
            {},
            far,
            {side: ((width, total), BF16) for side in "wx"},
            {},
            {},
            limit=2,
        )

    pieces = jnp.concatenate([biases, biases_other], axis=1)
    span = heads_half * 2 + hidden_half
    query_bias_all = jnp.concatenate([pieces[:, :heads_half], pieces[:, span : span + heads_half]], 1)
    value_bias_all = jnp.concatenate(
        [pieces[:, heads_half:features], pieces[:, span + heads_half : span + features]], 1
    )
    up_bias_all = jnp.concatenate([pieces[:, features:span], pieces[:, span + features :]], 1)

    def own_rows(value):
        start = (core * mine_rows,) + (0,) * (value.ndim - 1)
        return lax.dynamic_slice(value, start, (mine_rows,) + value.shape[1:])

    own_segments = own_rows(segments)
    same = own_segments[:, :, None] == own_segments[:, None, :]
    held = ("grad", "query", "key", "value", "probs", "normed2", "att", "factor2")
    held += ("act", "before", "grad_fed")
    masks = jnp.where(same, 0.0, MASKED).astype(F32)
    own_input = own_rows(activations)
    own_cotangent = own_rows(cotangent)

    act = ((tokens, width), BF16)
    state = ((tokens, width), F32)
    head = ((tokens, features), BF16)
    hid = ((tokens, hidden), BF16)
    column = ((tokens, 128), F32)
    probs_shape = ((heads, slots, slots), BF16)

    kept = [[None] * SAMPLE for _ in range(layers)]
    feed_sums = [[None] * SAMPLE for _ in range(layers)]
    for layer in range(layers):
        last = layer == layers - 1
        attend_weights = staged(layer, attend_names)
        for m in samples:
            near = dict(mask=masks[m], gain=first_gain, shift=first_shift)
            near.update(query_bias=query_bias_all, value_bias=value_bias_all)
            near.update(attend_weights)
            saved = dict(
                normed=act, query=head, key=head, value=head, probs=probs_shape, mixed=head
            )
            saved["factor"] = column
            if layer == 0:
                near["source"] = own_input[m]
            else:
                before = kept[layer - 1][m]
                near.update(middle=before["middle"], mine=before["fed_mine"])
                near.update(theirs=before["fed_theirs"], feed_scale=feed_scale, down_bias=down_bias)
                saved["fed"] = act
            inner = dict(current=state, part=act)
            if last:
                inner.update({name: saved.pop(name) for name in list(saved) if name in held})
            outs = run(
                chain,
                functools.partial(attend_forward, layer),
                6,
                near,
                {},
                inner,
                saved,
                {},
            )
            if layer > 0:
                before["fed"] = outs.pop("fed")
            kept[layer][m] = now = dict(outs)
            now["mine"], now["theirs"] = outs["part"], swap_x(outs["part"])
        feed_weights = staged(layer, feed_names)
        for m in samples:
            now = kept[layer][m]
            near = {name: now[name] for name in ("current", "mine", "theirs")}
            near.update(attend_scale=attend_scale, out_bias=out_bias, up_bias=up_bias_all)
            near.update(gain=second_gain, shift=second_shift)
            near.update(feed_weights)
            inner = dict(middle=state, part=act)
            saved = dict(normed2=act, att=act, factor2=column, act=hid)
            if not last:
                saved["slope"] = hid
                body = feed_forward
            else:
                near.update(grad=own_cotangent[m], feed_scale=feed_scale)
                del inner["middle"]
                inner.update(sums=((1, width), F32), wide_sums=((1, hidden), F32))
                saved.update(middle=state, fed_part=act, grad_fed=act, before=hid)
                inner.update({name: saved.pop(name) for name in list(saved) if name in held})
                body = feed_both
            outs = run(
                chain,
                functools.partial(body, layer),
                11 if last else 7,
                near,
                {},
                inner,
                saved,
                {},
            )
            now.update(outs)
            if not last:
                now["fed_mine"], now["fed_theirs"] = outs["part"], swap_x(outs["part"])
            else:
                now["mine"], now["theirs"] = outs["part"], swap_x(outs["part"])
                now["fed_mine"] = outs["fed_part"]
                now["grad"] = own_cotangent[m]
                feed_sums[layer][m] = (outs["sums"], outs["wide_sums"])

    me = lax.axis_index(DP)
    def order_of(bits):
        if not direct:
            return jnp.arange(8).astype(jnp.int32)
        a, b, c = bits
        keep = (b + c, b, c, 0)
        return (me ^ jnp.array([a + r for r in keep] + list(keep))).astype(jnp.int32)

    table = order_of((1, 2, 4))
    len_table = 8

    core_now = core.astype(jnp.int32).reshape(1)
    half_shape = ((width // 2, 4 * heads_half), BF16)
    assert hidden_half == 4 * heads_half

    def products(layer, groups, column=None, bulk=None, span=1, ways=((1, 2, 4),), parts=1):
        if not direct:
            ways = ways[:1]
        near, far, room, plan = {}, {}, {}, []
        for left, rights in groups:
            for name in [left, *rights]:
                for m in samples:
                    value = kept[layer][m][name]
                    if name in held and layer == layers - 1:
                        near[name + str(m)] = value
                    else:
                        far[name + FAR + str(m)] = value
                        room[name + str(m)] = (value.shape, BF16)
                        plan.append((name + FAR + str(m), name + str(m), None, None))
        if column is not None:
            return run(
                chain,
                with_loads(functools.partial(weight_grad, 8, 1, groups, column), plan),
                6,
                near,
                far,
                {},
                {},
                dict(room, block=((2 * width, 4 * heads_half), BF16)),
                table=core_now,
                whole=dict(bulk=((2 * width, span * hidden_half), BF16)),
                over=bulk,
            )["bulk"]
        outs = run(
            chain,
            with_loads(functools.partial(weight_grad, 8, len(ways), groups, None), plan),
            6,
            near,
            far,
            dict(own_send=half_shape),
            dict(
                {term(0, i): ((width // parts, 4 * heads_half), BF16) for i in range(parts)},
                own_keep=half_shape,
            ),
            room,
            table=jnp.concatenate([order_of(bits) for bits in ways]),
            limit=16,
        )
        outs["got"] = [swap_core(outs[term(0, i)]) for i in range(parts)]
        outs["ways"] = ways
        return outs

    quarter_shape = ((width // 4, 4 * heads_half), BF16)
    eighth_shape = ((width // 8, 4 * heads_half), BF16)

    def swap_dp(value, bit):
        return lax.ppermute(value, DP, [(i, i ^ bit) for i in range(n)])

    def depart(outs):
        total = run(
            chain,
            add_send,
            1,
            dict(
                {term(0, i): v for i, v in enumerate(outs["got"][: max(1, len(outs["got"]) // 2)])},
                own_send=outs["own_send"],
            ),
            {},
            {
                term(1, way): ((width // 2, 4 * heads_half // len(outs["ways"])), BF16)
                for way in range(len(outs["ways"]))
            },
            {},
            {},
            limit=4,
        )
        totals = [total[term(1, way)] for way in range(len(outs["ways"]))]
        if direct:
            totals = [swap_dp(value, bits[0]) for value, bits in zip(totals, outs["ways"])]
        outs["arrived"] = totals

    def second(outs):
        if not direct:
            return
        gots = outs["got"]
        late = gots[len(gots) // 2 :]
        far, loads, plan = dict(own_keep=outs["own_keep"]), dict(own_keep=half_shape), []
        for index, value in enumerate(late):
            far[term(0, index)] = value
            loads[term(0, index)] = ((width // 2 // len(late), 4 * heads_half), BF16)
        for name in far:
            part = slice(width // 2, width) if far[name].shape[0] == width else None
            plan.append((name + FAR, name, part, None))
        found = run(
            chain,
            with_loads(add_first, plan),
            2,
            {term(1, way): value for way, value in enumerate(outs["arrived"])},
            {name + FAR: value for name, value in far.items()},
            dict(
                {
                    term(2, way): ((width // 4, 4 * heads_half // len(outs["ways"])), BF16)
                    for way in range(len(outs["ways"]))
                },
                stay=quarter_shape,
            ),
            {},
            loads,
            limit=8,
        )
        outs["keep"] = found["stay"]
        outs["arrived"] = [
            swap_dp(found[term(2, way)], bits[1]) for way, bits in enumerate(outs["ways"])
        ]

    def third(outs):
        if not direct:
            return
        found = run(
            chain,
            add_second,
            1,
            dict(
                {term(1, way): value for way, value in enumerate(outs["arrived"])},
                keep=outs["keep"],
            ),
            {},
            dict(leave=eighth_shape, stay=eighth_shape),
            {},
            {},
            limit=4,
        )
        outs["keep"], outs["arrived"] = found["stay"], swap_dp(found["leave"], 4)

    def fourth(outs):
        if not direct:
            got = jnp.concatenate(outs["got"], axis=0)
            keep = outs["own_keep"].astype(F32) + got[width // 2 :].astype(F32)
            rows_now = jnp.concatenate([outs["arrived"][0].astype(F32), keep], axis=0)
            return lax.psum_scatter(rows_now, DP, scatter_dimension=0, tiled=True)
        return run(
            chain,
            add_third,
            1,
            dict(arrived=outs["arrived"], keep=outs["keep"]),
            {},
            {},
            dict(found=(eighth_shape[0], F32)),
            {},
            limit=4,
        )["found"]

    def assemble(found, names, each):
        if not direct:
            found[0] = [fourth(value) for value in found[0]]
            found[1] = [array[:, at : at + hidden_half].astype(F32) for array, at in found[1]]
            joined = jnp.stack([jnp.concatenate(pieces_now, axis=1) for pieces_now in found])
            return [joined[:, :, i * each : (i + 1) * each] for i in range(len(names))]
        near, far, loads, plan = {}, {}, {}, []
        for layer, pieces_now in enumerate(found):
            for piece_now, value in enumerate(pieces_now):
                if layer == 0:
                    near[term(layer, piece_now, 0)] = value["keep"]
                    near[term(layer, piece_now, 1)] = value["arrived"]
                    continue
                name = term(layer, piece_now, 0)
                array, column = value
                far[name + FAR] = array
                shape = (array.shape[0], hidden_half)
                loads[name] = (shape, BF16)
                part = (slice(None), slice(column, column + hidden_half))
                plan.append((name + FAR, name, part, None))
        outs = run(
            chain,
            with_loads(functools.partial(add_last, layers, len(found[0]), names), plan),
            3,
            near,
            far,
            {},
            {name: ((layers, eighth_shape[0][0], each), F32) for name in names},
            loads,
            limit=12,
        )
        return [outs[name] for name in names]

    up_group = [("normed2", ["before"])]
    down_group = [("grad_fed", ["act"])]
    attend_group = [("normed", ["gq", "gk", "gv"]), ("grad_att", ["mixed"])]
    attend_sums = [[None] * SAMPLE for _ in range(layers)]

    def back_feed(layer, m, weights):
        now, deep = kept[layer][m], kept[layer + 1][m]
        near = dict(mine=deep["mine"], theirs=deep["theirs"])
        near.update(gain=first_gain, shift=first_shift)
        near.update(feed_scale=feed_scale, down_bias=down_bias)
        near.update(weights)
        far = dict(normed_hbm=deep["normed"], factor_hbm=deep["factor"])
        far.update(after_hbm=deep["grad_middle"], fed_hbm=now["fed"], slope_hbm=now["slope"])
        loads = dict(normed=act, factor=column, after=state, fed=act, slope=hid)
        outs = run(
            chain,
            with_loads(
                functools.partial(feed_backward, layer),
                simple_plan(loads),
            ),
            8,
            near,
            far,
            dict(part=act, sums=((4, width), F32), wide_sums=((1, hidden), F32)),
            dict(grad=state, grad_fed=act, before=hid),
            loads,
        )
        now.update(outs)
        now["mine"], now["theirs"] = outs["part"], swap_x(outs["part"])
        feed_sums[layer][m] = (outs["sums"], outs["wide_sums"])

    def back_attend(layer, m, weights):
        now = kept[layer][m]
        near = dict(mine=now["mine"], theirs=now["theirs"])
        near.update(gain=second_gain, shift=second_shift)
        near.update(attend_scale=attend_scale, out_bias=out_bias)
        near.update(weights)
        far, loads = {}, {}
        sources = dict(normed2=act, factor2=column, grad=act if layer == layers - 1 else state)
        sources["att"] = act
        sources.update(value=head, probs=probs_shape, key=head, query=head)
        for name, shape in sources.items():
            if layer == layers - 1 and name in held:
                near[name] = now[name]
            else:
                far[name + FAR] = now[name]
                loads[name] = shape
        outs = run(
            chain,
            with_loads(
                functools.partial(attend_backward, layer),
                simple_plan(loads),
            ),
            7,
            near,
            far,
            dict(
                part=act,
                sums=((4, width), F32),
                wide_sums=((2, features), F32),
            ),
            dict(grad_middle=state, grad_att=act, gq=head, gk=head, gv=head),
            dict(loads, grad_mixed=head),
        )
        now.update(outs)
        now["mine"], now["theirs"] = outs["part"], swap_x(outs["part"])
        attend_sums[layer][m] = (outs["sums"], outs["wide_sums"])

    results, last_sums = [], []

    def finish_row(m):
        now = kept[layers - 1][m]
        mine, _ = lax.optimization_barrier((now["fed_mine"], kept[0][SAMPLE - 1]["grad_att"]))
        far = dict(mine_hbm=mine, theirs_hbm=swap_x(mine), middle_hbm=now["middle"])
        near = dict(grad=own_cotangent[m], feed_scale=feed_scale, down_bias=down_bias)
        outs = run(
            chain,
            with_loads(
                functools.partial(finish_forward, layers - 1),
                simple_plan(("mine", "theirs", "middle")),
            ),
            2,
            near,
            far,
            dict(result=act, sums=((1, width), F32)),
            {},
            dict(mine=act, theirs=act, middle=state),
        )
        results.append(outs["result"])
        last_sums.append(outs["sums"])


    inputs_grad, final_sums = [], []

    def final_row(m):
        now = kept[0][m]
        near = dict(mine=now["mine"], theirs=now["theirs"])
        near.update(gain=first_gain, shift=first_shift)
        loads = dict(normed=act, factor=column, after=state)
        now["after"] = now["grad_middle"]
        outs = run(
            chain,
            with_loads(
                finish_backward, simple_plan(loads)
            ),
            2,
            near,
            {name + FAR: now[name] for name in loads},
            dict(input_grad=state, sums=((2, width), F32)),
            {},
            loads,
        )
        inputs_grad.append(outs["input_grad"])
        final_sums.append(outs["sums"])

    def gather_vectors():
        near = {}
        for layer in range(layers):
            for m in samples:
                attend_rows, attend_wide = attend_sums[layer][m]
                feed_rows, feed_wide = feed_sums[layer][m]
                for index, value in enumerate((attend_rows, attend_wide, feed_rows, feed_wide)):
                    near[term(layer, index, m)] = value
        for m in samples:
            near[term(layers, 0, m)] = final_sums[m]
            near[term(layers, 1, m)] = last_sums[m]
        each = width // len_table
        small_shape = ((len_table, SMALL, each), F32)
        outs = run(
            chain,
            functools.partial(gather_small, layers, heads_half, hidden_half),
            1,
            near,
            {},
            dict(own=small_shape, give=small_shape),
            {},
            dict(common=((8 * layers, width), F32), up=((layers, hidden_half), F32)),
            table=table,
            limit=4,
        )
        return outs["own"], swap_core(outs["give"])

    def halve(keep, arrived, bit):
        if not direct:
            return keep, arrived
        rows_now = keep.shape[0] // 2
        shape = ((rows_now,) + keep.shape[1:], F32)
        found = run(
            chain,
            add_halves,
            1,
            dict(keep=keep, arrived=arrived),
            {},
            dict(leave=shape, stay=shape),
            {},
            {},
            limit=2,
        )
        return found["stay"], swap_dp(found["leave"], bit)

    def vector_grads(keep, arrived):
        each = width // len_table
        small = keep + arrived
        if direct:
            total = small[0]
            vectors = total[: 8 * layers].reshape(layers, 8, each)
            up_bias_grad = total[8 * layers : 9 * layers]
            wide = total[9 * layers :].reshape(-1)[: 4 * layers * each * 2]
        else:
            total = lax.psum(small, DP).transpose(1, 0, 2).reshape(SMALL, -1)
            mine = lax.dynamic_slice_in_dim(total, me * (width // n), width // n, 1)
            vectors = mine[: 8 * layers].reshape(layers, 8, width // n)
            up_bias_grad = mine[8 * layers : 9 * layers]
            wide = total[9 * layers :, :each].reshape(-1)[: 4 * layers * each * 2]
        wide = wide[: 2 * layers * heads_half].reshape(layers, 2, heads_half)
        wide = lax.dynamic_slice_in_dim(wide, me * (heads_half // n), heads_half // n, 2)
        query_bias_grad, value_bias_grad = wide[:, 0], wide[:, 1]
        return vectors, up_bias_grad, query_bias_grad, value_bias_grad

    def join(values):
        near = {term(0, m): values[m] for m in samples}
        near.update({term(1, m): swap_core(values[m]) for m in samples})
        return run(
            chain,
            place_rows,
            3,
            near,
            {},
            {},
            {},
            {},
            table=core_now,
            limit=2,
            whole=dict(whole=((rows, slots, width), values[0].dtype)),
        )["whole"]

    assert layers == 2
    bulk = products(1, up_group, 0, None, 2)
    bulk = products(1, down_group, hidden_half, bulk, 2)
    bulk = lax.psum_scatter(bulk, (CORE, DP), scatter_dimension=0, tiled=True)
    attend_weights1 = staged(1, attend_names)
    back_attend(1, 0, attend_weights1)
    back_attend(1, 1, attend_weights1)
    feed_weights0 = staged(0, feed_names)
    back_feed(0, 0, feed_weights0)
    back_feed(0, 1, feed_weights0)
    attend_weights0 = staged(0, attend_names)
    back_attend(0, 0, attend_weights0)
    back_attend(0, 1, attend_weights0)
    up0 = products(0, up_group, ways=((1, 2, 4),), parts=2)
    down0 = products(0, down_group, ways=((2, 1, 4),), parts=1)
    depart(up0)
    attend0 = products(0, attend_group, ways=((1, 2, 4),), parts=1)
    depart(down0)
    bulk_attend = products(1, attend_group, 0, None, 1)
    bulk_attend = lax.psum_scatter(bulk_attend, (CORE, DP), scatter_dimension=0, tiled=True)
    depart(attend0)
    second(up0)
    second(down0)
    final_row(0)
    final_row(1)
    finish_row(0)
    finish_row(1)
    small_keep, small_arrived = gather_vectors()
    third(up0)
    small_keep, small_arrived = halve(small_keep, small_arrived, 1)
    second(attend0)
    whole_grad = join(inputs_grad)
    third(down0)
    small_keep, small_arrived = halve(small_keep, small_arrived, 2)
    whole_result = join(results)
    third(attend0)
    found1 = [(bulk, 0), (bulk, hidden_half)]
    up_grad, down_grad = assemble([[up0, down0], found1], ("up", "down"), hidden_half)
    small_keep, small_arrived = halve(small_keep, small_arrived, 4)
    q_grad, k_grad, v_grad, o_grad = assemble(
        [[attend0], [(bulk_attend, 0)]], ("query", "key", "value", "out"), heads_half
    )
    vectors, up_bias_grad, query_bias_grad, value_bias_grad = vector_grads(
        small_keep, small_arrived
    )
    return (
        whole_result,
        whole_grad,
        vectors[:, 0],
        vectors[:, 1],
        q_grad,
        k_grad,
        v_grad,
        query_bias_grad,
        value_bias_grad,
        o_grad,
        vectors[:, 2],
        vectors[:, 3],
        vectors[:, 4],
        vectors[:, 5],
        up_grad,
        up_bias_grad,
        down_grad,
        vectors[:, 6],
        vectors[:, 7],
    )


def solution(mesh):
    split = Mesh(mesh.devices.reshape(mesh.shape[DP], 2, 2), (DP,) + SHARED)
    return jax.shard_map(
        functools.partial(per_device, mesh.shape[DP]),
        mesh=split,
        in_specs=(
            P(DP, None, None),
            P(DP, None),
            P(),
            P(),
            P(None, None, SHARED),
            P(None, None, SHARED),
            P(None, None, SHARED),
            P(None, SHARED),
            P(None, SHARED),
            P(None, None, SHARED),
            P(),
            P(),
            P(),
            P(),
            P(None, None, SHARED),
            P(None, SHARED),
            P(None, None, SHARED),
            P(),
            P(),
            P(DP, None, None),
        ),
        out_specs=(
            P(DP, None, None),
            P(DP, None, None),
            P(None, DP),
            P(None, DP),
            P(None, DP, SHARED),
            P(None, DP, SHARED),
            P(None, DP, SHARED),
            P(None, SHARED + (DP,)),
            P(None, SHARED + (DP,)),
            P(None, DP, SHARED),
            P(None, DP),
            P(None, DP),
            P(None, DP),
            P(None, DP),
            P(None, DP, SHARED),
            P(None, SHARED + (DP,)),
            P(None, DP, SHARED),
            P(None, DP),
            P(None, DP),
        ),
        check_vma=False,
    )
```
